32 devices in a mesh: segment: 4 (over y, x), seq: 8 (over z, core).
Axes of the slice: x: 2, y: 2, z: 4, core: 2. Of those that a mesh axis runs over, the one named last changes fastest.
Arguments:
- held: bfloat16 [4, 1024, 1024], P('segment', 'seq'), may hold values from -6 to 6
- log_decay: float32 [4, 1024, 8], P('segment', 'seq'), may hold values from -2 to 0, as said below
- route_ids: int32 [4, 8, 1], P('segment'), may hold values from 0 to 7; in each aligned block of 8 rows (0 to 7, 8 to 15, ..., all dimensions but the last counted through in order) at most 2 rows name the same one
- norm_gain: float32 [4, 1024], P('segment'), may hold values from 0.1 to 1.9
- qkv_weight: bfloat16 [4, 1024, 3072], P('segment'), may hold values from -0.1875 to 0.1875
- beta_weight: bfloat16 [4, 1024, 8], P('segment'), may hold values from -0.1875 to 0.1875
- out_gain: float32 [4, 128], P('segment'), may hold values from 0.1 to 1.9
- out_weight: bfloat16 [4, 1024, 1024], P('segment'), may hold values from -0.1875 to 0.1875
- ffn_gain: float32 [4, 1024], P('segment'), may hold values from 0.1 to 1.9
- gate_weight: bfloat16 [4, 8, 1024, 4096], P('segment', 'seq'), may hold values from -0.1875 to 0.1875
- up_weight: bfloat16 [4, 8, 1024, 4096], P('segment', 'seq'), may hold values from -0.1875 to 0.1875
- down_weight: bfloat16 [4, 8, 4096, 1024], P('segment', 'seq'), may hold values from -0.09375 to 0.09375
Outputs:
- next_held: bfloat16 [4, 1024, 1024], P('segment', 'seq')
The draws below stay inside these ranges and needn't reach their ends.
Inputs may be any that keep to these rules, and one draw needn't show every extreme that they name: `log_decay`: every entry is negative. `route_ids`: within each aligned group of 8 consecutive blocks of a section no machine type is named more than 2 times, and in some group of every draw one type is named exactly 2 times.
All inputs are finite; a program needn't handle non-finite values.
Results may differ from the reference program's by a relative error of at most 0.018.
Values may be sent and summed in bfloat16 or wider, within the bound.
No kernel may reach another device: no remote copies, remote signals or barrier semaphores. Data moves between devices by JAX's collectives and lax.ppermute only.
A program may use at most 192 MiB of HBM per device.

```python
import math
from functools import partial
import jax
import jax.numpy as jnp
import numpy as np
from jax import lax

D = 1024
ATTENTION_GROUPS = 8
HEAD = 128
FF = 4096
EXPERTS = 8
BLOCK = 128
TOK_DEV = 128
RELAY_LEGS = 4
MOMENT_TOTAL = 1024
NBLOCKS = 8
SLICES = 1
FF_SLICE = 4096
SHARDS = 8
GROUP_BLOCKS = 8
CAP = 2


def draw_log_decay(key, part):
    lookup_vectors = jax.random.split(key, 8)
    fast_share = 0.5
    rough = jax.random.uniform(lookup_vectors[0], (RELAY_LEGS, MOMENT_TOTAL, ATTENTION_GROUPS), jnp.float32, 0.5, 1.5)
    fast = jax.random.uniform(lookup_vectors[1], (RELAY_LEGS, 1, ATTENTION_GROUPS), jnp.float32) < fast_share
    fast_rate = jnp.exp(jax.random.uniform(lookup_vectors[2], (RELAY_LEGS, 1, ATTENTION_GROUPS), jnp.float32, jnp.log(2.0), jnp.log(4.0))) / BLOCK
    slow_rate = jnp.exp(jax.random.uniform(lookup_vectors[3], (RELAY_LEGS, 1, ATTENTION_GROUPS), jnp.float32, jnp.log(0.1), jnp.log(0.25))) / MOMENT_TOTAL
    rate = jnp.where(fast, fast_rate, slow_rate)
    device_factor = jnp.exp(jax.random.uniform(lookup_vectors[4], (RELAY_LEGS, MOMENT_TOTAL // TOK_DEV, 1, ATTENTION_GROUPS), jnp.float32, jnp.log(0.5), jnp.log(2.0)))
    device_factor = jnp.broadcast_to(device_factor, (RELAY_LEGS, MOMENT_TOTAL // TOK_DEV, TOK_DEV, ATTENTION_GROUPS)).reshape(RELAY_LEGS, MOMENT_TOTAL, ATTENTION_GROUPS)
    anchor_index = -rate * rough * device_factor
    leading_packet = jax.random.randint(lookup_vectors[5], (RELAY_LEGS, 1, 1, ATTENTION_GROUPS), 0, MOMENT_TOTAL)
    initial_shift = jax.random.randint(lookup_vectors[7], (RELAY_LEGS, 1, 1, ATTENTION_GROUPS), 1, MOMENT_TOTAL)
    trailing_packet = (leading_packet + initial_shift) % MOMENT_TOTAL
    packet_locus = jnp.concatenate([leading_packet, trailing_packet], axis=2)
    stratum_level = jnp.log(jax.random.uniform(lookup_vectors[6], (RELAY_LEGS, 1, 2, ATTENTION_GROUPS), jnp.float32, 0.55, 0.8))
    moment_number = jnp.arange(MOMENT_TOTAL).reshape(1, MOMENT_TOTAL, 1, 1)
    symbol_packet = jnp.sum(jnp.where(moment_number == packet_locus, stratum_level, 0.0), axis=2)
    return (anchor_index + symbol_packet).astype(jnp.float32)


def shard_levels(stream_key, dims, cuts, smallest, top_value):
    factor_of = 1.0
    for dim, shards_of in cuts:
        steps = jax.random.uniform(jax.random.fold_in(jax.random.fold_in(stream_key, 6), dim), (shards_of,), jnp.float32, smallest / len(cuts), top_value / len(cuts))
        factor_of = factor_of * jnp.repeat(jnp.exp(steps), dims[dim] // shards_of).reshape((-1,) + (1,) * (len(dims) - 1 - dim))
    return factor_of


def routed_block(own_key, own, number, rows, amount, top, most, lean):
    sequence = jax.random.permutation(own_key, amount)
    heavy_load, usual = shares(amount, rows * top, most, lean, True), shares(amount, rows * top, most, lean, False)
    places = jnp.arange(amount)

    def named(lengths, offset_by):
        used = int((lengths > 0).sum())
        fixed = max(1, used // 4)
        shifted = fixed + (places - fixed + offset_by * (used - fixed)) % max(1, amount - fixed)
        return jnp.zeros((amount,), jnp.int32).at[sequence[jnp.where(places < fixed, places, shifted)]].set(jnp.asarray(lengths, jnp.int32))

    lengths = jnp.where(number % 4 == 0, named(heavy_load, number // 4), named(usual, number - number // 4 - 1))
    mixed = jax.random.permutation(jax.random.fold_in(own, 3), amount)
    donor, sink = mixed[0:amount // 2 * 2:2], mixed[1:amount // 2 * 2:2]
    slack = jnp.minimum(lengths[donor] - 1, most - lengths[sink]) // 2
    slack = jnp.where((donor == sequence[0]) | (sink == sequence[0]) | (lengths[sink] == 0), 0, jnp.maximum(slack, 0))
    shifted = jax.random.randint(jax.random.fold_in(own, 4), (amount // 2,), 0, 1 << 20) % (slack + 1)
    lengths = lengths.at[donor].add(-shifted).at[sink].add(shifted)
    members = jnp.searchsorted(jnp.cumsum(lengths), jnp.arange(rows * top), side="right").astype(jnp.int32)
    table = members.reshape(top, rows).T
    table = table[jax.random.permutation(jax.random.fold_in(own, 1), rows)]
    offset_by = jax.random.randint(jax.random.fold_in(own, 2), (rows, 1), 0, top)
    return jnp.take_along_axis(table, (jnp.arange(top)[None, :] + offset_by) % top, axis=1)


def shares(number_of, total, reach, lean, full):
    portions = [(1 << 20) // math.isqrt(standing ** lean) + 1 for standing in range(1, number_of + 1)]
    largest = reach if full else min(reach, max(-(-total // number_of), total * portions[0] // sum(portions)))
    least = 1 if total - largest >= number_of - 1 else 0
    holding, rest = [largest] + [least] * (number_of - 1), total - largest - least * (number_of - 1)
    while rest > 0:
        candidates = [i for i in range(1, number_of) if holding[i] < largest] or [i for i in range(1, number_of) if holding[i] < reach]
        mass, remaining = sum([portions[i] for i in candidates]), rest
        for i in candidates:
            extra = min(reach - holding[i], max(1, remaining * portions[i] // mass), rest)
            holding[i] = holding[i] + extra
            rest = rest - extra
    return np.array(holding)


def gaussian(stream_key, dims, width, most, cuts=(), held_as=jnp.bfloat16):
    array = jax.random.normal(stream_key, dims, jnp.float32) * width
    if len(cuts) > 0:
        array = shard_levels(stream_key, dims, cuts, -0.22, 0.18) * array
    return jnp.clip(array, min=-most, max=most).astype(held_as)


def setup_inputs(seed: int = 0) -> dict:
    seeds = jax.random.split(jax.random.key(seed), 13)
    held = gaussian(seeds[0], (RELAY_LEGS, MOMENT_TOTAL, D), 1.0, 6.0, ((0, 4), (1, 8)))
    log_decay = draw_log_decay(jax.random.fold_in(seeds[12], 71), 0)
    route_ids_keys = jax.random.split(jax.random.fold_in(seeds[2], 1), RELAY_LEGS * NBLOCKS // GROUP_BLOCKS)
    route_ids_turns = jax.random.permutation(jax.random.fold_in(seeds[2], 3), RELAY_LEGS * NBLOCKS // GROUP_BLOCKS)
    route_ids = jax.vmap(lambda own, number: routed_block(jax.random.fold_in(seeds[2], 2), own, number, GROUP_BLOCKS, EXPERTS, 1, CAP, 2))(route_ids_keys, route_ids_turns).reshape((RELAY_LEGS, NBLOCKS, 1))
    norm_gain = jnp.clip(1.0 + 0.18 * jax.random.normal(seeds[3], (RELAY_LEGS, D), jnp.float32), 0.1, 1.9)
    qkv_weight = gaussian(seeds[4], (RELAY_LEGS, D, 3 * D), D ** -0.5, 0.1875, ((0, 4),))
    beta_weight = gaussian(seeds[5], (RELAY_LEGS, D, ATTENTION_GROUPS), D ** -0.5, 0.1875, ((0, 4),))
    out_gain = jnp.clip(1.0 + 0.18 * jax.random.normal(seeds[6], (RELAY_LEGS, HEAD), jnp.float32), 0.1, 1.9)
    out_weight = gaussian(seeds[7], (RELAY_LEGS, D, D), D ** -0.5, 0.1875, ((0, 4),))
    ffn_gain = jnp.clip(1.0 + 0.18 * jax.random.normal(seeds[8], (RELAY_LEGS, D), jnp.float32), 0.1, 1.9)
    gate_weight = gaussian(seeds[9], (RELAY_LEGS, SHARDS, D, FF_SLICE), D ** -0.5, 0.1875, ((0, 4), (1, 8)))
    up_weight = gaussian(seeds[10], (RELAY_LEGS, SHARDS, D, FF_SLICE), D ** -0.5, 0.1875, ((0, 4), (1, 8)))
    down_weight = gaussian(seeds[11], (RELAY_LEGS, SHARDS, FF_SLICE, D), FF ** -0.5, 0.09375, ((0, 4), (1, 8)))
    return dict(held=held, log_decay=log_decay, route_ids=route_ids, norm_gain=norm_gain, qkv_weight=qkv_weight, beta_weight=beta_weight, out_gain=out_gain, out_weight=out_weight, ffn_gain=ffn_gain, gate_weight=gate_weight, up_weight=up_weight, down_weight=down_weight)


def rms(values, gain):
    return values * lax.rsqrt(lax.optimization_barrier(jnp.mean(values * values, axis=-1, keepdims=True)) + 1e-06) * gain

def unit_lower_solve(strict_part, rhs):
    ein = partial(jnp.einsum, precision=lax.Precision.HIGHEST)
    length = strict_part.shape[-1]
    raised = -strict_part
    running = jnp.eye(length, dtype=jnp.float32) + raised
    for _ in range((length - 1).bit_length() - 1):
        raised = ein('hij,hjk->hik', raised, raised)
        running = running + ein('hij,hjk->hik', running, raised)
    return ein('hij,hjk->hik', running, rhs)

def span_terms(lookup_vectors, values, beta, logd):
    ein = partial(jnp.einsum, precision=lax.Precision.HIGHEST)
    length = lookup_vectors.shape[1]
    dim_k = lookup_vectors.shape[2]
    cumul = jnp.cumsum(logd, axis=-1)
    posit = jnp.arange(length)
    strict = posit[:, None] > posit[None, :]
    differ = cumul[:, :, None] - cumul[:, None, :]
    ratio = jnp.where(strict, jnp.exp(jnp.where(strict, differ, 0.0)), 0.0)
    inner = ein('htd,hsd->hts', lookup_vectors, lookup_vectors)
    strict_part = beta[:, :, None] * ratio * inner
    growth = jnp.exp(cumul)
    rhs = jnp.concatenate([(beta * growth)[:, :, None] * lookup_vectors, beta[:, :, None] * values], axis=-1)
    solved = unit_lower_solve(strict_part, rhs)
    w_part = solved[..., :dim_k]
    u_part = solved[..., dim_k:]
    tail = jnp.exp(cumul[:, -1:] - cumul)
    scaled = tail[:, :, None] * lookup_vectors
    trans_a = growth[:, -1][:, None, None] * jnp.eye(dim_k, dtype=jnp.float32) - ein('hck,hcj->hkj', w_part, scaled)
    trans_b = ein('hcv,hck->hvk', u_part, scaled)
    return (cumul, w_part, u_part, trans_a, trans_b)

def span_output(queries, lookup_vectors, cumul, w_part, u_part, state):
    ein = partial(jnp.einsum, precision=lax.Precision.HIGHEST)
    length = lookup_vectors.shape[1]
    posit = jnp.arange(length)
    incl = posit[:, None] >= posit[None, :]
    differ = cumul[:, :, None] - cumul[:, None, :]
    ratio = jnp.where(incl, jnp.exp(jnp.where(incl, differ, 0.0)), 0.0)
    update = u_part - ein('hck,hvk->hcv', w_part, state)
    scores = ein('htd,hsd->hts', queries, lookup_vectors) * ratio
    return jnp.exp(cumul)[:, :, None] * ein('hck,hvk->hcv', queries, state) + ein('hts,hsv->htv', scores, update)

def one_section(x, logd, ids, norm_g, w_qkv, w_beta, out_g, w_out, ffn_g, w_gate, w_up, w_down):
    ein = partial(jnp.einsum, precision=lax.Precision.HIGHEST)
    xf = x.astype(jnp.float32)
    xn = rms(xf, norm_g).astype(jnp.bfloat16)
    qkv = jnp.dot(xn, w_qkv, preferred_element_type=jnp.float32).astype(jnp.bfloat16).astype(jnp.float32)
    queries = qkv[:, :D].reshape(MOMENT_TOTAL, ATTENTION_GROUPS, HEAD)
    lookup_vectors = qkv[:, D:2 * D].reshape(MOMENT_TOTAL, ATTENTION_GROUPS, HEAD)
    values = qkv[:, 2 * D:].reshape(MOMENT_TOTAL, ATTENTION_GROUPS, HEAD)
    queries = queries * lax.rsqrt(lax.optimization_barrier(jnp.sum(queries * queries, axis=-1, keepdims=True)) + 1e-06)
    lookup_vectors = lookup_vectors * lax.rsqrt(lax.optimization_barrier(jnp.sum(lookup_vectors * lookup_vectors, axis=-1, keepdims=True)) + 1e-06)
    beta = jax.nn.sigmoid(jnp.dot(xn, w_beta, preferred_element_type=jnp.float32))
    spans = MOMENT_TOTAL // BLOCK

    def arrange(arr):
        return arr.reshape(spans, BLOCK, ATTENTION_GROUPS, HEAD).transpose(0, 2, 1, 3)
    q_c = arrange(queries)
    k_c = arrange(lookup_vectors)
    v_c = arrange(values)
    b_c = beta.reshape(spans, BLOCK, ATTENTION_GROUPS).transpose(0, 2, 1)
    l_c = logd.reshape(spans, BLOCK, ATTENTION_GROUPS).transpose(0, 2, 1)

    def advance(state, pieces):
        q_one, k_one, v_one, b_one, l_one = pieces
        cumul, w_part, u_part, trans_a, trans_b = span_terms(k_one, v_one, b_one, l_one)
        result = span_output(q_one, k_one, cumul, w_part, u_part, state)
        return (ein('hvk,hkj->hvj', state, trans_a) + trans_b, result)
    start = jnp.zeros((ATTENTION_GROUPS, HEAD, HEAD), jnp.float32)
    final, outs = lax.scan(advance, start, (q_c, k_c, v_c, b_c, l_c))
    mixed = outs.transpose(0, 2, 1, 3).reshape(MOMENT_TOTAL, ATTENTION_GROUPS, HEAD)
    normed = rms(mixed, out_g).astype(jnp.bfloat16).reshape(MOMENT_TOTAL, D)
    hidden = (xf + jnp.dot(normed, w_out, preferred_element_type=jnp.float32)).astype(jnp.bfloat16)
    hn = rms(hidden.astype(jnp.float32), ffn_g).astype(jnp.bfloat16)
    blocks = hn.reshape(NBLOCKS, BLOCK, D)

    def expert_block(args):
        rows, kind = args
        index = (jnp.arange(SLICES) * EXPERTS + kind).astype(jnp.int32)
        gate_all = jnp.take(w_gate, index, axis=0).transpose(1, 0, 2).reshape(D, SLICES * FF_SLICE)
        up_all = jnp.take(w_up, index, axis=0).transpose(1, 0, 2).reshape(D, SLICES * FF_SLICE)
        down_all = jnp.take(w_down, index, axis=0).reshape(SLICES * FF_SLICE, D)
        gate = jnp.dot(rows, gate_all, preferred_element_type=jnp.float32)
        up_val = jnp.dot(rows, up_all, preferred_element_type=jnp.float32)
        act = (jax.nn.silu(gate) * up_val).astype(jnp.bfloat16)
        return jnp.dot(act, down_all, preferred_element_type=jnp.float32).astype(jnp.bfloat16)
    ffn = lax.map(expert_block, (blocks, ids[:, 0])).reshape(MOMENT_TOTAL, D)
    return (hidden.astype(jnp.float32) + ffn.astype(jnp.float32)).astype(jnp.bfloat16)

def reference(held, log_decay, route_ids, norm_gain, qkv_weight, beta_weight, out_gain, out_weight, ffn_gain, gate_weight, up_weight, down_weight):
    outs = []
    for section in range(RELAY_LEGS):
        outs.append(one_section(held[section], log_decay[section], route_ids[section], norm_gain[section], qkv_weight[section], beta_weight[section], out_gain[section], out_weight[section], ffn_gain[section], gate_weight[section], up_weight[section], down_weight[section]))
    stacked = jnp.stack(outs, axis=0)
    return jnp.roll(stacked, 1, axis=0)
```

```python
from functools import partial

import jax
import jax.numpy as jnp
from jax import lax
from jax.experimental import pallas as pl
from jax.experimental.pallas import tpu as pltpu
from jax.sharding import PartitionSpec as P

EXPERTS = 8
BLOCK = 128
CHIPS = 4
CORES = 2
CAP = 2
F32 = jnp.float32
BF16 = jnp.bfloat16
VMEM_LIMIT = 56 * 1024 * 1024


def lane_route(count, hop):
    route = []
    for i in range(count):
        base, chip, core = i - i % EXPERTS, i % EXPERTS // CORES, i % CORES
        route.append((i, base + (chip + hop) % CHIPS * CORES + core))
    return route


def pair_route(count):
    return [(i, i ^ 1) for i in range(count)]


def chip_route(count, k):
    return [(i, i ^ (CORES * k)) for i in range(count)]


def home_route(sections, count, k):
    return [
        (s * count + i, (s + 1) % sections * count + (i ^ (CORES * k)))
        for s in range(sections)
        for i in range(count)
    ]


def mm(a, b, dims=((1,), (0,))):
    return lax.dot_general(a, b, (dims, ((), ())), preferred_element_type=F32)


def halves(a):
    high = a.astype(BF16)
    return high, (a - high.astype(F32)).astype(BF16)


def mm3(a, b):
    (ah, al), (bh, bl) = a, b
    return mm(ah, bh) + (mm(ah, bl) + mm(al, bh))


def place_iota():
    row = lax.broadcasted_iota(jnp.int32, (BLOCK, BLOCK), 0)
    col = lax.broadcasted_iota(jnp.int32, (BLOCK, BLOCK), 1)
    return row, col


def lower_inverse(negs):
    row, col = place_iota()
    eye = jnp.where(row == col, 1.0, 0.0).astype(F32)
    small = 16
    near = row // small == col // small
    diag = [jnp.where(near, n, 0.0) for n in negs]
    total = [eye + d for d in diag]
    power = [halves(d) for d in diag]
    for _ in range((small - 1).bit_length() - 1):
        power = [halves(mm3(p, p)) for p in power]
        total = [t + mm3(halves(t), p) for t, p in zip(total, power)]
    size = small
    while size < BLOCK:
        off = (row // (2 * size) == col // (2 * size)) & (row // size != col // size)
        cross = [halves(jnp.where(off, n, 0.0)) for n in negs]
        split = [halves(t) for t in total]
        left = [halves(mm3(t, c)) for t, c in zip(split, cross)]
        total = [t + mm3(m, s) for t, m, s in zip(total, left, split)]
        size *= 2
    return total


def unit(v):
    return v * lax.rsqrt(jnp.sum(v * v, axis=-1, keepdims=True) + 1e-06)


def running_decay(logd_ref, cum_ref):
    row, col = place_iota()
    upto = jnp.where(row <= col, 1.0, 0.0).astype(BF16)
    rest = logd_ref[...]
    total = jnp.zeros_like(rest)
    for _ in range(3):
        part = rest.astype(BF16)
        total = total + mm(part, upto)
        rest = rest - part.astype(F32)
    cum_ref[...] = total


def block_terms(projs, cums):
    row, col = place_iota()
    hd = BLOCK
    q = [unit(p[:, :hd].astype(BF16).astype(F32)) for p in projs]
    k = [unit(p[:, hd : 2 * hd].astype(BF16).astype(F32)) for p in projs]
    v = [p[:, 2 * hd : 3 * hd].astype(BF16).astype(F32) for p in projs]
    beta = [jax.nn.sigmoid(p[:, 3 * hd :]) for p in projs]
    across = [jnp.broadcast_to(c, (BLOCK, BLOCK)) for c in cums]
    down = [jnp.transpose(a) for a in across]
    kb = [a.astype(BF16) for a in k]
    inner = [
        mm(jnp.concatenate([a.astype(BF16), b], axis=0), b, ((1,), (1,))) for a, b in zip(q, kb)
    ]
    ratio = [
        jnp.where(row >= col, jnp.exp(jnp.where(row >= col, d - a, 0.0)), 0.0)
        for d, a in zip(down, across)
    ]
    negs = [
        jnp.where(row > col, -(b * r * i[BLOCK:]), 0.0) for b, r, i in zip(beta, ratio, inner)
    ]
    growth = [jnp.exp(d) for d in down]
    rhs = [
        jnp.concatenate([b * g * a, b * c], axis=1) for b, g, a, c in zip(beta, growth, k, v)
    ]
    inv = lower_inverse(negs)
    solved = [mm3(halves(t), halves(r)).astype(BF16) for t, r in zip(inv, rhs)]
    scores = [(i[:BLOCK] * r).astype(BF16) for i, r in zip(inner, ratio)]
    inside = [mm(s, w) for s, w in zip(scores, solved)]
    last = [d[BLOCK - 1 :, :] for d in down]
    tail = [(jnp.exp(e - d) * a).astype(BF16) for e, d, a in zip(last, down, k)]
    step = [mm(w, t, ((0,), (0,))) for w, t in zip(solved, tail)]
    fade = [jnp.exp(e) for e in last]
    reads = [g * a - i[:, :hd] for g, a, i in zip(growth, q, inside)]
    local = [i[:, hd:] for i in inside]
    return reads, local, step, fade


def arrivals(place):
    chip, core = place // CORES % CHIPS, place % CORES
    return [
        (chip + hop) % CHIPS * CORES + (core if side == 0 else 1 - core)
        for hop in (0, 3, 1, 2)
        for side in (0, 1)
    ]


def terms_kernel(first, count, meta_ref, logd_ref, gain_ref, weight_ref, *refs):
    x_refs = refs[:count]
    reads_ref, local_ref, step_ref, fade_ref, cum_ref, norm_ref = refs[count:]
    running_decay(logd_ref, cum_ref)
    blocks = arrivals(meta_ref[0])[first : first + count]
    gain = gain_ref[...]
    for j in range(count):
        xf = x_refs[j][...].astype(F32)
        scale = lax.rsqrt(jnp.mean(xf * xf, axis=-1, keepdims=True) + 1e-06)
        norm_ref[j * BLOCK : (j + 1) * BLOCK, :] = (xf * scale * gain).astype(BF16)
    for j in range(0, count, 2):
        both = mm(norm_ref[j * BLOCK : (j + 2) * BLOCK, :], weight_ref[...])
        reads, local, step, fade = block_terms(
            [both[:BLOCK], both[BLOCK:]], [cum_ref[pl.ds(blocks[i], 1), :] for i in (j, j + 1)]
        )
        for i in range(2):
            reads_ref[j + i] = reads[i].astype(BF16)
            local_ref[j + i] = local[i]
            step_ref[j + i] = step[i]
            fade_ref[j + i] = jnp.broadcast_to(fade[i], (8, BLOCK))


def terms(first, meta, logd, gain, weight, blocks):
    count = len(blocks)
    width = blocks[0].shape[1]
    vmem = pl.BlockSpec(memory_space=pltpu.VMEM)
    return pl.pallas_call(
        partial(terms_kernel, first, count),
        out_shape=(
            jax.ShapeDtypeStruct((count, BLOCK, BLOCK), BF16),
            jax.ShapeDtypeStruct((count, BLOCK, BLOCK), F32),
            jax.ShapeDtypeStruct((count, 2 * BLOCK, BLOCK), F32),
            jax.ShapeDtypeStruct((count, 8, BLOCK), F32),
        ),
        in_specs=[pl.BlockSpec(memory_space=pltpu.SMEM)] + [vmem] * (3 + count),
        out_specs=(vmem,) * 4,
        scratch_shapes=[
            pltpu.VMEM((EXPERTS, BLOCK), F32),
            pltpu.VMEM((count * BLOCK, width), BF16),
        ],
        compiler_params=pltpu.CompilerParams(vmem_limit_bytes=VMEM_LIMIT),
        cost_estimate=pl.CostEstimate(
            flops=count * 2 * BLOCK * (width * 512 + 60 * BLOCK * BLOCK),
            bytes_accessed=count * 800000 + 2000000,
            transcendentals=count * 60000,
        ),
        name="chunk_terms",
    )(meta, logd, gain, weight, *blocks)


def mix_kernel(early, late, meta_ref, start_ref, gain_ref, *refs):
    first = refs[:4]
    second = refs[4:8]
    outs = refs[8 : 8 + CHIPS]
    reads_scr, local_scr, step_scr, fade_scr, on_scr = refs[8 + CHIPS :]
    place = meta_ref[0]
    blocks = arrivals(place)
    for group, at, count in ((first, 0, early), (second, early, late)):
        for j in range(count):
            spot = blocks[at + j]
            for ref, scr in zip(group, (reads_scr, local_scr, step_scr, fade_scr)):
                scr[spot] = ref[j]
    state = start_ref[...]
    gain = gain_ref[...]
    for b in range(EXPERTS):
        split = halves(state)
        move = step_scr[b]
        mixed = mm(reads_scr[b], split[0], ((1,), (1,))) + local_scr[b]
        scale = lax.rsqrt(jnp.mean(mixed * mixed, axis=-1, keepdims=True) + 1e-06)
        on_scr[b] = (mixed * scale * gain).astype(BF16)
        if b + 1 < EXPERTS:
            erase = mm3(split, halves(move[:BLOCK]))
            state = fade_scr[b][0:1, :] * state - erase + move[BLOCK:]
    chip = place // CORES % CHIPS
    for k in range(CHIPS):
        there = jnp.bitwise_xor(chip, k)
        for side in range(CORES):
            for slot in range(CAP):
                source = meta_ref[1 + (there * CORES + side) * CAP + slot]
                outs[k][side, slot] = on_scr[source]


def mix(meta, start, gain, first, second):
    early, late = first[0].shape[0], second[0].shape[0]
    vmem = pl.BlockSpec(memory_space=pltpu.VMEM)
    sent = jax.ShapeDtypeStruct((CORES, CAP, BLOCK, BLOCK), BF16)
    return pl.pallas_call(
        partial(mix_kernel, early, late),
        out_shape=(sent,) * CHIPS,
        in_specs=[pl.BlockSpec(memory_space=pltpu.SMEM)] + [vmem] * 10,
        out_specs=(vmem,) * CHIPS,
        scratch_shapes=[
            pltpu.VMEM((EXPERTS, BLOCK, BLOCK), BF16),
            pltpu.VMEM((EXPERTS, BLOCK, BLOCK), F32),
            pltpu.VMEM((EXPERTS, 2 * BLOCK, BLOCK), F32),
            pltpu.VMEM((EXPERTS, 8, BLOCK), F32),
            pltpu.VMEM((EXPERTS, BLOCK, BLOCK), BF16),
        ],
        compiler_params=pltpu.CompilerParams(vmem_limit_bytes=VMEM_LIMIT),
        name="state_walk",
    )(meta, start, gain, *first, *second)


def project(meta_ref, gain_ref, out_weight_ref, x_ref, on_refs, on_scr, h_ref, hn_ref):
    place = meta_ref[0]
    chip, core = place // CORES % CHIPS, place % CORES
    for k in range(CHIPS):
        there = jnp.bitwise_xor(chip, k)
        for side in range(CORES):
            head = there * CORES + (core if side == 0 else 1 - core)
            at = pl.ds(pl.multiple_of(head * BLOCK, BLOCK), BLOCK)
            got = on_refs[k * CORES + side]
            for slot in range(CAP):
                on_scr[slot * BLOCK : (slot + 1) * BLOCK, at] = got[core, slot]
    hidden = x_ref[...].astype(F32) + mm(on_scr[...], out_weight_ref[...])
    hidden = hidden.astype(BF16)
    h_ref[...] = hidden
    hf = hidden.astype(F32)
    scale = lax.rsqrt(jnp.mean(hf * hf, axis=-1, keepdims=True) + 1e-06)
    hn_ref[...] = (hf * scale * gain_ref[...]).astype(BF16)


def project_kernel(meta_ref, gain_ref, out_weight_ref, x_ref, *refs):
    on_refs = refs[: CHIPS * CORES]
    h_ref, hn_ref, on_scr = refs[CHIPS * CORES :]
    project(meta_ref, gain_ref, out_weight_ref, x_ref, on_refs, on_scr, h_ref, hn_ref)


def expert_kernel(meta_ref, gain_ref, out_weight_ref, x_ref, gate_ref, up_ref, down_ref, *refs):
    on_refs = refs[: CHIPS * CORES]
    out_ref, on_scr, h_scr, hn_scr, sum_scr = refs[CHIPS * CORES :]
    at = pl.program_id(0)

    @pl.when(at == 0)
    def _():
        project(meta_ref, gain_ref, out_weight_ref, x_ref, on_refs, on_scr, h_scr, hn_scr)
        sum_scr[...] = jnp.zeros_like(sum_scr)

    rows = hn_scr[...]
    gate = mm(rows, gate_ref[0, 0])
    up = mm(rows, up_ref[0, 0])
    act = (gate / (1.0 + jnp.exp(-gate)) * up).astype(BF16)
    sum_scr[...] += mm(act, down_ref[0, 0])

    @pl.when(at == pl.num_programs(0) - 1)
    def _():
        ffn = sum_scr[...].astype(BF16).astype(F32)
        out_ref[...] = (h_scr[...].astype(F32) + ffn).astype(BF16)


def expert(meta, gain, out_weight, x_rows, gate, up, down, ons):
    rows, width = x_rows.shape
    hidden = gate.shape[3]
    tile = min(512, hidden)
    vmem = pl.BlockSpec(memory_space=pltpu.VMEM)
    return pl.pallas_call(
        expert_kernel,
        out_shape=jax.ShapeDtypeStruct((rows, width), BF16),
        grid=(hidden // tile,),
        in_specs=[pl.BlockSpec(memory_space=pltpu.SMEM), vmem, vmem, vmem]
        + [pl.BlockSpec((1, 1, width, tile), lambda i: (0, 0, 0, i))] * 2
        + [pl.BlockSpec((1, 1, tile, width), lambda i: (0, 0, i, 0))]
        + [vmem] * len(ons),
        out_specs=vmem,
        scratch_shapes=[
            pltpu.VMEM((rows, width), BF16),
            pltpu.VMEM((rows, width), BF16),
            pltpu.VMEM((rows, width), BF16),
            pltpu.VMEM((rows, width), F32),
        ],
        compiler_params=pltpu.CompilerParams(vmem_limit_bytes=VMEM_LIMIT),
        name="expert",
    )(meta, gain, out_weight, x_rows, gate, up, down, *ons)


def project_only(meta, gain, out_weight, x_rows, ons):
    rows, width = x_rows.shape
    vmem = pl.BlockSpec(memory_space=pltpu.VMEM)
    return pl.pallas_call(
        project_kernel,
        out_shape=(jax.ShapeDtypeStruct((rows, width), BF16),) * 2,
        in_specs=[pl.BlockSpec(memory_space=pltpu.SMEM)] + [vmem] * (3 + len(ons)),
        out_specs=(vmem, vmem),
        scratch_shapes=[pltpu.VMEM((rows, width), BF16)],
        compiler_params=pltpu.CompilerParams(vmem_limit_bytes=VMEM_LIMIT),
        name="project",
    )(meta, gain, out_weight, x_rows, *ons)


def group_start(place, count, first, second):
    groups = count // EXPERTS
    ein = partial(jnp.einsum, precision=lax.Precision.HIGHEST)
    eye = jnp.eye(BLOCK, dtype=F32)
    step = jnp.concatenate([first[2], second[2]], axis=0)
    fade = jnp.concatenate([first[3], second[3]], axis=0)
    order = jnp.argsort(jnp.stack(arrivals(place)))
    step, fade = jnp.take(step, order, axis=0), jnp.take(fade, order, axis=0)
    moves = fade[:, 0, :][:, None, :] * eye - step[:, :BLOCK]
    adds = step[:, BLOCK:]
    total, added = moves[0], adds[0]
    for b in range(1, EXPERTS):
        total, added = ein("ij,jk->ik", total, moves[b]), ein("vk,kj->vj", added, moves[b]) + adds[b]
    peers = [[g * EXPERTS + e for g in range(groups)] for e in range(EXPERTS)]
    gather = partial(lax.all_gather, axis_name="seq", axis_index_groups=peers)
    totals, addeds = gather(total), gather(added)

    def one(hop, state):
        return ein(
            "vk,kj->vj", state, lax.dynamic_index_in_dim(totals, hop, 0, False)
        ) + lax.dynamic_index_in_dim(addeds, hop, 0, False)

    return lax.fori_loop(0, place // EXPERTS, one, jnp.zeros((BLOCK, BLOCK), F32))


def per_device(
    held,
    log_decay,
    route_ids,
    norm_gain,
    qkv_weight,
    beta_weight,
    out_gain,
    out_weight,
    ffn_gain,
    gate_weight,
    up_weight,
    down_weight,
):
    count = lax.axis_size("seq")
    sections = lax.axis_size("segment")
    groups = count // EXPERTS
    place = lax.axis_index("seq")
    group, inner = place // EXPERTS, place % EXPERTS
    chip, core = inner // CORES, inner % CORES
    width = held.shape[2]
    pair = partial(lax.ppermute, axis_name="seq", perm=pair_route(count))

    def hop(block, by):
        return lax.ppermute(block, "seq", lane_route(count, by))

    own = held[0]
    left = hop(own, 1)
    right = hop(own, -1)
    far = hop(left, 1)
    near = [own, pair(own), left, pair(left), right, pair(right)]
    distant = [far, pair(far)]

    members = [[g * EXPERTS + e for e in range(EXPERTS)] for g in range(groups)]
    decays = lax.all_gather(
        log_decay[0].T, "seq", axis_index_groups=members if groups > 1 else None
    )
    decays = lax.dynamic_index_in_dim(decays, inner, 1, False)

    def head_columns(at):
        return lax.dynamic_slice_in_dim(qkv_weight[0], at * width + inner * BLOCK, BLOCK, 1)

    beta_column = lax.dynamic_slice_in_dim(beta_weight[0], inner, 1, 1)
    weight = jnp.concatenate(
        [head_columns(0), head_columns(1), head_columns(2)]
        + [jnp.broadcast_to(beta_column, (width, BLOCK))],
        axis=1,
    )

    kinds = lax.dynamic_slice_in_dim(route_ids[0, :, 0], group * EXPERTS, EXPERTS)
    index = jnp.arange(EXPERTS)
    same = kinds[:, None] == kinds[None, :]
    rank = jnp.sum((same & (index[None, :] < index[:, None])).astype(jnp.int32), axis=1)
    named = (kinds[None, None, :] == index[:, None, None]) & (
        rank[None, None, :] == jnp.arange(CAP)[None, :, None]
    )
    source = jnp.sum(jnp.where(named, index[None, None, :], 0), axis=2).astype(jnp.int32)
    meta = jnp.concatenate([place.astype(jnp.int32)[None], source.reshape(-1)])

    first = terms(0, meta, decays, norm_gain, weight, near)
    second = terms(6, meta, decays, norm_gain, weight, distant)
    if groups > 1:
        start = group_start(place, count, first, second)
    else:
        start = jnp.zeros((BLOCK, BLOCK), F32)
    sends = mix(meta, start, out_gain, first, second)

    got = [sends[0]] + [lax.ppermute(sends[k], "seq", chip_route(count, k)) for k in range(1, CHIPS)]
    ons = []
    for block in got:
        ons += [block, pair(block)]

    stacked = jnp.stack(near + distant, axis=0)
    wanted = lax.dynamic_index_in_dim(source, inner, 0, False)
    hop_index = jnp.array([0, 4, 6, 2], jnp.int32)
    came = jnp.take(hop_index, (wanted // CORES - chip) % CHIPS) + (wanted % CORES != core)
    x_rows = jnp.take(stacked, came, axis=0).reshape(CAP * BLOCK, width)

    if groups == 1:
        finished = expert(
            meta, ffn_gain, out_weight[0], x_rows, gate_weight, up_weight, down_weight, ons
        )
    else:
        hidden, hn = project_only(meta, ffn_gain, out_weight[0], x_rows, ons)
        peers = [[g * EXPERTS + e for g in range(groups)] for e in range(EXPERTS)]
        rows = lax.all_gather(hn, "seq", axis_index_groups=peers, tiled=True)
        gate = jnp.dot(rows, gate_weight[0, 0], preferred_element_type=F32)
        up = jnp.dot(rows, up_weight[0, 0], preferred_element_type=F32)
        act = (jax.nn.silu(gate) * up).astype(BF16)
        part = jnp.dot(act, down_weight[0, 0], preferred_element_type=F32)
        ffn = lax.psum_scatter(
            part, "seq", scatter_dimension=0, axis_index_groups=peers, tiled=True
        ).astype(BF16)
        finished = (hidden.astype(F32) + ffn.astype(F32)).astype(BF16)

    other = pair(finished)
    fronts = [finished[:BLOCK], finished[BLOCK:], other[:BLOCK], other[BLOCK:]]
    total = None
    for k in range(CHIPS):
        home = jnp.bitwise_xor(inner, CORES * k)
        kind = lax.dynamic_index_in_dim(kinds, home, 0, False)
        slot = lax.dynamic_index_in_dim(rank, home, 0, False)
        which = jnp.where(
            kind // CORES == chip, (kind % CORES != core).astype(jnp.int32) * CAP + slot, -1
        )
        send = jnp.zeros((BLOCK, width), BF16)
        for at, front in enumerate(fronts):
            send = jnp.where(which == at, front, send)
        moved = lax.ppermute(send, ("segment", "seq"), home_route(sections, count, k))
        total = moved if total is None else total + moved
    return total[None]


def solution(mesh):
    placed = (
        P("segment", "seq", None),
        P("segment", "seq", None),
        P("segment", None, None),
        P("segment", None),
        P("segment", None, None),
        P("segment", None, None),
        P("segment", None),
        P("segment", None, None),
        P("segment", None),
        P("segment", "seq", None, None),
        P("segment", "seq", None, None),
        P("segment", "seq", None, None),
    )
    return jax.shard_map(
        per_device, mesh=mesh, in_specs=placed, out_specs=P("segment", "seq", None), check_vma=False
    )
```

```python
from functools import partial

import jax
import jax.numpy as jnp
from jax import lax
from jax.experimental import pallas as pl
from jax.experimental.pallas import tpu as pltpu
from jax.sharding import PartitionSpec as P

EXPERTS = 8
BLOCK = 128
CHIPS = 4
CORES = 2
CAP = 2
PARTS = 3
EXTRA = 16
F32 = jnp.float32
BF16 = jnp.bfloat16
VMEM_LIMIT = 16 * 1024 * 1024


def lane_route(count, hop):
    route = []
    for i in range(count):
        base, chip, core = i - i % EXPERTS, i % EXPERTS // CORES, i % CORES
        route.append((i, base + (chip + hop) % CHIPS * CORES + core))
    return route


def pair_route(count):
    return [(i, i ^ 1) for i in range(count)]


def chip_route(count, k):
    return [(i, i ^ (CORES * k)) for i in range(count)]


def home_route(sections, count, hop):
    return [
        (s * count + i, (s + 1) % sections * count + j)
        for s in range(sections)
        for i, j in lane_route(count, hop)
    ]


def mm(a, b, dims=((1,), (0,))):
    return lax.dot_general(a, b, (dims, ((), ())), preferred_element_type=F32)


def halves(a):
    high = a.astype(BF16)
    return high, (a - high.astype(F32)).astype(BF16)


def mm3(a, b):
    (ah, al), (bh, bl) = a, b
    return mm(ah, bh) + (mm(ah, bl) + mm(al, bh))


def place_iota():
    row = lax.broadcasted_iota(jnp.int32, (BLOCK, BLOCK), 0)
    col = lax.broadcasted_iota(jnp.int32, (BLOCK, BLOCK), 1)
    return row, col


def lower_inverse(negs):
    row, col = place_iota()
    eye = jnp.where(row == col, 1.0, 0.0).astype(F32)
    small = 16
    near = row // small == col // small
    diag = [jnp.where(near, n, 0.0) for n in negs]
    total = [eye + d for d in diag]
    power = [d.astype(BF16) for d in diag]
    for _ in range((small - 1).bit_length() - 1):
        power = [mm(p, p).astype(BF16) for p in power]
        total = [t + mm(t.astype(BF16), p) for t, p in zip(total, power)]
    size = small
    while size < BLOCK:
        off = (row // (2 * size) == col // (2 * size)) & (row // size != col // size)
        cross = [jnp.where(off, n, 0.0).astype(BF16) for n in negs]
        short = [t.astype(BF16) for t in total]
        left = [mm(t, c).astype(BF16) for t, c in zip(short, cross)]
        total = [t + mm(m, s) for t, m, s in zip(total, left, short)]
        size *= 2
    return total


def unit(v):
    return v * lax.rsqrt(jnp.sum(v * v, axis=-1, keepdims=True) + 1e-06)


def attach_kernel(x_ref, decay_ref, out_ref, sem):
    copy = pltpu.make_async_copy(x_ref, out_ref.at[pl.ds(0, BLOCK), :], sem)
    copy.start()
    rest = decay_ref[...]
    heads = rest.shape[0]
    row = lax.broadcasted_iota(jnp.int32, (EXTRA, BLOCK), 0)
    parts = []
    for _ in range(PARTS):
        parts.append(rest.astype(BF16).astype(F32))
        rest = rest - parts[-1]
    for h in range(heads):
        block = jnp.zeros((EXTRA, BLOCK), F32)
        for n, part in enumerate(parts):
            block = jnp.where(row == n, part[h : h + 1, :], block)
        out_ref[BLOCK:, h * BLOCK : (h + 1) * BLOCK] = block.astype(BF16)
    copy.wait()


def attach(x, decay):
    vmem = pl.BlockSpec(memory_space=pltpu.VMEM)
    return pl.pallas_call(
        attach_kernel,
        out_shape=jax.ShapeDtypeStruct((BLOCK + EXTRA, x.shape[1]), BF16),
        in_specs=[pl.BlockSpec(memory_space=pl.ANY), vmem],
        out_specs=vmem,
        scratch_shapes=[pltpu.SemaphoreType.DMA],
        compiler_params=pltpu.CompilerParams(vmem_limit_bytes=VMEM_LIMIT),
        name="attach_decay",
    )(x, decay)


def running_decay(parts):
    row, col = place_iota()
    upto = jnp.where(row <= col, 1.0, 0.0).astype(BF16)
    return jnp.sum(mm(parts, upto), axis=0, keepdims=True)


def block_terms(projs, cums):
    row, col = place_iota()
    hd = BLOCK
    q = [unit(p[:, :hd].astype(BF16).astype(F32)) for p in projs]
    k = [unit(p[:, hd : 2 * hd].astype(BF16).astype(F32)) for p in projs]
    v = [p[:, 2 * hd : 3 * hd].astype(BF16).astype(F32) for p in projs]
    beta = [jax.nn.sigmoid(p[:, 3 * hd :]) for p in projs]
    across = [jnp.broadcast_to(c, (BLOCK, BLOCK)) for c in cums]
    down = [jnp.transpose(a) for a in across]
    kb = [a.astype(BF16) for a in k]
    inner = [
        mm(jnp.concatenate([a.astype(BF16), b], axis=0), b, ((1,), (1,))) for a, b in zip(q, kb)
    ]
    ratio = [
        jnp.where(row >= col, jnp.exp(jnp.where(row >= col, d - a, 0.0)), 0.0)
        for d, a in zip(down, across)
    ]
    negs = [
        jnp.where(row > col, -(b * r * i[BLOCK:]), 0.0) for b, r, i in zip(beta, ratio, inner)
    ]
    growth = [jnp.exp(d) for d in down]
    rhs = [
        jnp.concatenate([b * g * a, b * c], axis=1) for b, g, a, c in zip(beta, growth, k, v)
    ]
    inv = lower_inverse(negs)
    solved = [mm(t.astype(BF16), r.astype(BF16)).astype(BF16) for t, r in zip(inv, rhs)]
    scores = [(i[:BLOCK] * r).astype(BF16) for i, r in zip(inner, ratio)]
    inside = [mm(s, w) for s, w in zip(scores, solved)]
    last = [d[BLOCK - 1 :, :] for d in down]
    tail = [(jnp.exp(e - d) * a).astype(BF16) for e, d, a in zip(last, down, k)]
    step = [mm(w, t, ((0,), (0,))) for w, t in zip(solved, tail)]
    fade = [jnp.exp(e) for e in last]
    reads = [g * a - i[:, :hd] for g, a, i in zip(growth, q, inside)]
    local = [i[:, hd:] for i in inside]
    return reads, local, step, fade


def where_am_i():
    place = lax.axis_index("seq")
    inner = jnp.bitwise_and(place, EXPERTS - 1)
    return place - inner, inner // CORES, jnp.bitwise_and(inner, 1)


def routes(kinds_ref, base):
    kinds = [kinds_ref[base + b] for b in range(EXPERTS)]
    ranks = []
    for b in range(EXPERTS):
        rank = jnp.int32(0)
        for earlier in range(b):
            rank = rank + jnp.where(kinds[earlier] == kinds[b], 1, 0)
        ranks.append(rank)
    return kinds, ranks


def sources(kinds, ranks, kind):
    found = []
    for slot in range(CAP):
        block = jnp.int32(0)
        for b in range(EXPERTS):
            block = block + jnp.where((kinds[b] == kind) & (ranks[b] == slot), b, 0)
        found.append(block)
    return found


def arrivals(chip, core):
    return [
        jnp.bitwise_and(chip + hop, CHIPS - 1) * CORES + (core if side == 0 else 1 - core)
        for hop in (0, 3, 1, 2)
        for side in (0, 1)
    ]


def normed(x, gain):
    xf = x.astype(F32)
    return (xf * lax.rsqrt(jnp.mean(xf * xf, axis=-1, keepdims=True) + 1e-06) * gain).astype(BF16)


def pair_terms(gain_ref, weight_ref, x_refs, norm_ref, put):
    _, chip, core = where_am_i()
    at = pl.ds(pl.multiple_of((chip * CORES + core) * BLOCK, BLOCK), BLOCK)
    gain = gain_ref[...]
    for j, ref in enumerate(x_refs):
        norm_ref[j * BLOCK : (j + 1) * BLOCK, :] = normed(ref[:BLOCK, :], gain)
    both = mm(norm_ref[...], weight_ref[...])
    reads, local, step, fade = block_terms(
        [both[:BLOCK], both[BLOCK:]], [running_decay(ref[BLOCK:, at]) for ref in x_refs]
    )
    for i in range(len(x_refs)):
        put(i, reads[i].astype(BF16), local[i], step[i], jnp.broadcast_to(fade[i], (8, BLOCK)))


def term_scratch(count, width):
    return [pltpu.VMEM((count * BLOCK, width), BF16)]


def term_shapes(count):
    return (
        ((count, BLOCK, BLOCK), BF16),
        ((count, BLOCK, BLOCK), F32),
        ((count, 2 * BLOCK, BLOCK), F32),
        ((count, 8, BLOCK), F32),
    )


def terms_kernel(gain_ref, weight_ref, left_ref, right_ref, *refs):
    outs, scratch = refs[:4], refs[4:]

    def put(j, *values):
        for ref, value in zip(outs, values):
            ref[j] = value

    pair_terms(gain_ref, weight_ref, (left_ref, right_ref), *scratch, put)


def terms(gain, weight, blocks):
    count = len(blocks)
    width = blocks[0].shape[1]
    vmem = pl.BlockSpec(memory_space=pltpu.VMEM)
    return pl.pallas_call(
        terms_kernel,
        out_shape=tuple(jax.ShapeDtypeStruct(*s) for s in term_shapes(count)),
        in_specs=[vmem] * 4,
        out_specs=(vmem,) * 4,
        scratch_shapes=term_scratch(count, width),
        compiler_params=pltpu.CompilerParams(vmem_limit_bytes=VMEM_LIMIT),
        cost_estimate=pl.CostEstimate(
            flops=4 * 10**9, bytes_accessed=3 * 10**6, transcendentals=10**5
        ),
        name="chunk_terms",
    )(gain, weight, *blocks)


def mix_kernel(counts, late, kinds_ref, out_gain_ref, *refs):
    base, chip, core = where_am_i()
    blocks = arrivals(chip, core)
    groups = [refs[4 * g : 4 * g + 4] for g in range(len(counts))]
    refs = refs[4 * len(counts) :]
    if late:
        gain_ref, weight_ref, left_ref, right_ref = refs[:4]
        refs = refs[4:]
    else:
        start_ref, refs = refs[0], refs[1:]
    outs, refs = refs[:CHIPS], refs[CHIPS:]
    scr, on_scr, refs = refs[:4], refs[4], refs[5:]
    at = 0
    for group, count in zip(groups, counts):
        for j in range(count):
            for ref, keep in zip(group, scr):
                keep[blocks[at]] = ref[j]
            at += 1
    if late:

        def put(j, *values):
            for ref, value in zip(scr, values):
                ref[blocks[at + j]] = value

        pair_terms(gain_ref, weight_ref, (left_ref, right_ref), *refs, put)
    reads_scr, local_scr, step_scr, fade_scr = scr
    state = jnp.zeros((BLOCK, BLOCK), F32) if late else start_ref[...]
    out_gain = out_gain_ref[...]
    for b in range(EXPERTS):
        split = halves(state)
        move = step_scr[b]
        mixed = mm(reads_scr[b], split[0], ((1,), (1,))) + local_scr[b]
        on_scr[b] = normed(mixed, out_gain)
        if b + 1 < EXPERTS:
            erase = mm3(split, halves(move[:BLOCK]))
            state = fade_scr[b][0:1, :] * state - erase + move[BLOCK:]
    kinds, ranks = routes(kinds_ref, base)
    for k in range(CHIPS):
        there = jnp.bitwise_xor(chip, k)
        for side in range(CORES):
            found = sources(kinds, ranks, there * CORES + side)
            for slot in range(CAP):
                outs[k][side, slot] = on_scr[found[slot]]


def mix(kinds, out_gain, groups, start=None, late=()):
    counts = tuple(g[0].shape[0] for g in groups)
    vmem = pl.BlockSpec(memory_space=pltpu.VMEM)
    extra = list(late) if late else [start]
    operands = [kinds, out_gain] + [a for g in groups for a in g] + extra
    sent = jax.ShapeDtypeStruct((CORES, CAP, BLOCK, BLOCK), BF16)
    return pl.pallas_call(
        partial(mix_kernel, counts, bool(late)),
        out_shape=(sent,) * CHIPS,
        in_specs=[pl.BlockSpec(memory_space=pltpu.SMEM)] + [vmem] * (len(operands) - 1),
        out_specs=(vmem,) * CHIPS,
        scratch_shapes=[pltpu.VMEM(*s) for s in term_shapes(EXPERTS)]
        + [pltpu.VMEM((EXPERTS, BLOCK, BLOCK), BF16)]
        + (term_scratch(2, late[2].shape[1]) if late else []),
        compiler_params=pltpu.CompilerParams(vmem_limit_bytes=VMEM_LIMIT),
        cost_estimate=pl.CostEstimate(
            flops=3 * 10**10, bytes_accessed=4 * 10**6, transcendentals=10**5
        ),
        name="state_walk",
    )(*operands)


def home_kernel(kinds_ref, own_ref, other_ref, *outs):
    base, chip, core = where_am_i()
    kinds, ranks = routes(kinds_ref, base)
    for k in range(CHIPS):
        home = jnp.bitwise_and(chip + k, CHIPS - 1) * CORES + core
        kind, rank = jnp.int32(0), jnp.int32(0)
        for b in range(EXPERTS):
            kind = kind + jnp.where(home == b, kinds[b], 0)
            rank = rank + jnp.where(home == b, ranks[b], 0)
        here = kind // CORES == chip
        mine = jnp.bitwise_and(kind, 1) == core
        outs[k][...] = jnp.zeros_like(outs[k])
        for slot in range(CAP):
            rows = slice(slot * BLOCK, (slot + 1) * BLOCK)

            @pl.when(here & mine & (rank == slot))
            def _():
                outs[k][...] = own_ref[rows, :]

            @pl.when(here & jnp.logical_not(mine) & (rank == slot))
            def _():
                outs[k][...] = other_ref[rows, :]


def homeward(kinds, own, other):
    vmem = pl.BlockSpec(memory_space=pltpu.VMEM)
    rows, width = own.shape
    return pl.pallas_call(
        home_kernel,
        out_shape=(jax.ShapeDtypeStruct((rows // CAP, width), BF16),) * CHIPS,
        in_specs=[pl.BlockSpec(memory_space=pltpu.SMEM), vmem, vmem],
        out_specs=(vmem,) * CHIPS,
        compiler_params=pltpu.CompilerParams(vmem_limit_bytes=VMEM_LIMIT),
        name="homeward",
    )(kinds, own, other)


def project(kinds_ref, gain_ref, out_weight_ref, x_refs, on_refs, x_scr, on_scr, h_ref, hn_ref, sem):
    base, chip, core = where_am_i()
    kinds, ranks = routes(kinds_ref, base)
    found = sources(kinds, ranks, chip * CORES + core)
    for slot in range(CAP):
        for block, ref in zip(arrivals(chip, core), x_refs):

            @pl.when(block == found[slot])
            def _():
                rows = ref.at[pl.ds(0, BLOCK), :]
                pltpu.make_async_copy(rows, x_scr.at[slot], sem.at[slot]).start()

    for k in range(CHIPS):
        there = jnp.bitwise_xor(chip, k)
        for side in range(CORES):
            head = there * CORES + (core if side == 0 else 1 - core)
            at = pl.ds(pl.multiple_of(head * BLOCK, BLOCK), BLOCK)
            got = on_refs[k * CORES + side]
            for slot in range(CAP):
                on_scr[slot * BLOCK : (slot + 1) * BLOCK, at] = got[core, slot]
    for slot in range(CAP):
        rows = slice(slot * BLOCK, (slot + 1) * BLOCK)
        added = mm(on_scr[rows, :], out_weight_ref[...])
        rows_of_x = x_refs[0].at[pl.ds(0, BLOCK), :]
        pltpu.make_async_copy(rows_of_x, x_scr.at[slot], sem.at[slot]).wait()
        hidden = (x_scr[slot].astype(F32) + added).astype(BF16)
        h_ref[rows, :] = hidden
        hn_ref[rows, :] = normed(hidden, gain_ref[...])


def project_kernel(kinds_ref, gain_ref, out_weight_ref, *refs):
    x_refs, on_refs = refs[:EXPERTS], refs[EXPERTS : 2 * EXPERTS]
    h_ref, hn_ref, x_scr, on_scr, sem = refs[2 * EXPERTS :]
    project(kinds_ref, gain_ref, out_weight_ref, x_refs, on_refs, x_scr, on_scr, h_ref, hn_ref, sem)


def expert_kernel(tile, kinds_ref, gain_ref, out_weight_ref, *refs):
    x_refs, on_refs = refs[:EXPERTS], refs[EXPERTS : 2 * EXPERTS]
    gate_ref, up_ref, down_ref, out_ref = refs[2 * EXPERTS : 2 * EXPERTS + 4]
    x_scr, on_scr, h_scr, hn_scr, act_scr, sem = refs[2 * EXPERTS + 4 :]
    project(
        kinds_ref, gain_ref, out_weight_ref, x_refs, on_refs, x_scr, on_scr, h_scr, hn_scr, sem
    )
    rows = hn_scr[...]
    for at in range(0, gate_ref.shape[3], tile):
        part = slice(at, at + tile)
        gate = mm(rows, gate_ref[0, 0, :, part])
        up = mm(rows, up_ref[0, 0, :, part])
        act_scr[:, part] = (gate / (1.0 + jnp.exp(-gate)) * up).astype(BF16)
    width = out_ref.shape[1]
    for at in range(0, width, width // 2):
        part = slice(at, at + width // 2)
        ffn = mm(act_scr[...], down_ref[0, 0, :, part]).astype(BF16).astype(F32)
        out_ref[:, part] = (h_scr[:, part].astype(F32) + ffn).astype(BF16)


def expert(kinds, gain, out_weight, blocks, ons, gate, up, down):
    rows, width = CAP * BLOCK, blocks[0].shape[1]
    vmem = pl.BlockSpec(memory_space=pltpu.VMEM)
    return pl.pallas_call(
        partial(expert_kernel, min(512, gate.shape[3])),
        out_shape=jax.ShapeDtypeStruct((rows, width), BF16),
        in_specs=[pl.BlockSpec(memory_space=pltpu.SMEM), vmem, vmem]
        + [pl.BlockSpec(memory_space=pl.ANY)] * EXPERTS
        + [vmem] * (EXPERTS + 3),
        out_specs=vmem,
        scratch_shapes=[
            pltpu.VMEM((CAP, BLOCK, width), BF16),
            pltpu.VMEM((rows, width), BF16),
            pltpu.VMEM((rows, width), BF16),
            pltpu.VMEM((rows, width), BF16),
            pltpu.VMEM((rows, gate.shape[3]), BF16),
            pltpu.SemaphoreType.DMA((CAP,)),
        ],
        compiler_params=pltpu.CompilerParams(vmem_limit_bytes=VMEM_LIMIT),
        name="expert",
    )(kinds, gain, out_weight, *blocks, *ons, gate, up, down)


def project_only(kinds, gain, out_weight, blocks, ons):
    rows, width = CAP * BLOCK, blocks[0].shape[1]
    vmem = pl.BlockSpec(memory_space=pltpu.VMEM)
    return pl.pallas_call(
        project_kernel,
        out_shape=(jax.ShapeDtypeStruct((rows, width), BF16),) * 2,
        in_specs=[pl.BlockSpec(memory_space=pltpu.SMEM), vmem, vmem]
        + [pl.BlockSpec(memory_space=pl.ANY)] * EXPERTS
        + [vmem] * EXPERTS,
        out_specs=(vmem, vmem),
        scratch_shapes=[
            pltpu.VMEM((CAP, BLOCK, width), BF16),
            pltpu.VMEM((rows, width), BF16),
            pltpu.SemaphoreType.DMA((CAP,)),
        ],
        compiler_params=pltpu.CompilerParams(vmem_limit_bytes=VMEM_LIMIT),
        name="project",
    )(kinds, gain, out_weight, *blocks, *ons)


def group_start(place, count, groups_of_terms):
    groups = count // EXPERTS
    ein = partial(jnp.einsum, precision=lax.Precision.HIGHEST)
    eye = jnp.eye(BLOCK, dtype=F32)
    step = jnp.concatenate([g[2] for g in groups_of_terms], axis=0)
    fade = jnp.concatenate([g[3] for g in groups_of_terms], axis=0)
    inner = place % EXPERTS
    order = jnp.argsort(jnp.stack(arrivals(inner // CORES, inner % CORES)))
    step, fade = jnp.take(step, order, axis=0), jnp.take(fade, order, axis=0)
    moves = fade[:, 0, :][:, None, :] * eye - step[:, :BLOCK]
    adds = step[:, BLOCK:]
    total, added = moves[0], adds[0]
    for b in range(1, EXPERTS):
        total, added = ein("ij,jk->ik", total, moves[b]), ein("vk,kj->vj", added, moves[b]) + adds[b]
    peers = [[g * EXPERTS + e for g in range(groups)] for e in range(EXPERTS)]
    gather = partial(lax.all_gather, axis_name="seq", axis_index_groups=peers)
    totals, addeds = gather(total), gather(added)

    def one(hop, state):
        return ein(
            "vk,kj->vj", state, lax.dynamic_index_in_dim(totals, hop, 0, False)
        ) + lax.dynamic_index_in_dim(addeds, hop, 0, False)

    return lax.fori_loop(0, place // EXPERTS, one, jnp.zeros((BLOCK, BLOCK), F32))


def per_device(
    held,
    log_decay,
    route_ids,
    norm_gain,
    qkv_weight,
    beta_weight,
    out_gain,
    out_weight,
    ffn_gain,
    gate_weight,
    up_weight,
    down_weight,
):
    count = lax.axis_size("seq")
    sections = lax.axis_size("segment")
    groups = count // EXPERTS
    place = lax.axis_index("seq")
    inner = place % EXPERTS
    width = held.shape[2]
    pair = partial(lax.ppermute, axis_name="seq", perm=pair_route(count))
    kinds = route_ids.reshape(-1)

    def hop(block, by):
        return lax.ppermute(block, "seq", lane_route(count, by))

    own = attach(held[0], log_decay[0].T)
    left = hop(own, 1)
    own_other = pair(own)
    later, _ = lax.optimization_barrier((own, own_other))
    right = hop(later, -1)

    def head_columns(at):
        return lax.dynamic_slice_in_dim(qkv_weight[0], at * width + inner * BLOCK, BLOCK, 1)

    beta_column = lax.dynamic_slice_in_dim(beta_weight[0], inner, 1, 1)
    weight = jnp.concatenate(
        [head_columns(0), head_columns(1), head_columns(2)]
        + [jnp.broadcast_to(beta_column, (width, BLOCK))],
        axis=1,
    )

    known = [terms(norm_gain, weight, (own, own_other))]
    left, _ = lax.optimization_barrier((left, known[0][0]))
    far = hop(left, 1)
    near = [(own, own_other), (left, pair(left))]
    known.append(terms(norm_gain, weight, near[1]))
    near.append((right, pair(right)))
    known.append(terms(norm_gain, weight, near[2]))
    far, *_ = lax.optimization_barrier((far, known[1][0], known[2][0]))
    last = (far, pair(far))
    if groups > 1:
        known.append(terms(norm_gain, weight, last))
        sends = mix(kinds, out_gain, known, start=group_start(place, count, known))
    else:
        sends = mix(kinds, out_gain, known, late=(norm_gain, weight, *last))

    got = [sends[0]] + [lax.ppermute(sends[k], "seq", chip_route(count, k)) for k in range(1, CHIPS)]
    ons = []
    for block in got:
        ons += [block, pair(block)]
    blocks = [block for two in near + [last] for block in two]

    if groups == 1:
        finished = expert(
            kinds, ffn_gain, out_weight[0], blocks, ons, gate_weight, up_weight, down_weight
        )
    else:
        hidden, hn = project_only(kinds, ffn_gain, out_weight[0], blocks, ons)
        peers = [[g * EXPERTS + e for g in range(groups)] for e in range(EXPERTS)]
        rows = lax.all_gather(hn, "seq", axis_index_groups=peers, tiled=True)
        gate = jnp.dot(rows, gate_weight[0, 0], preferred_element_type=F32)
        up = jnp.dot(rows, up_weight[0, 0], preferred_element_type=F32)
        act = (jax.nn.silu(gate) * up).astype(BF16)
        part = jnp.dot(act, down_weight[0, 0], preferred_element_type=F32)
        ffn = lax.psum_scatter(
            part, "seq", scatter_dimension=0, axis_index_groups=peers, tiled=True
        ).astype(BF16)
        finished = (hidden.astype(F32) + ffn.astype(F32)).astype(BF16)

    def send_home(block, by):
        return lax.ppermute(block, ("segment", "seq"), home_route(sections, count, by))

    here, right_home, far_home, left_home = homeward(kinds, finished, pair(finished))
    passed = hop(far_home, 1)
    from_right = send_home(left_home, -1)
    from_here = send_home(here, 0)
    from_left = send_home(passed + right_home, 1)
    return (from_left + from_right + from_here)[None]


def solution(mesh):
    placed = (
        P("segment", "seq", None),
        P("segment", "seq", None),
        P("segment", None, None),
        P("segment", None),
        P("segment", None, None),
        P("segment", None, None),
        P("segment", None),
        P("segment", None, None),
        P("segment", None),
        P("segment", "seq", None, None),
        P("segment", "seq", None, None),
        P("segment", "seq", None, None),
    )
    return jax.shard_map(
        per_device, mesh=mesh, in_specs=placed, out_specs=P("segment", "seq", None), check_vma=False
    )
```

```python
from functools import partial

import jax
import jax.numpy as jnp
from jax import lax
from jax.experimental import pallas as pl
from jax.experimental.pallas import tpu as pltpu
from jax.sharding import PartitionSpec as P

EXPERTS = 8
BLOCK = 128
CHIPS = 4
CORES = 2
CAP = 2
PARTS = 3
EXTRA = 32
F32 = jnp.float32
BF16 = jnp.bfloat16
VMEM_LIMIT = 16 * 1024 * 1024


def lane_route(count, hop):
    route = []
    for i in range(count):
        base, chip, core = i - i % EXPERTS, i % EXPERTS // CORES, i % CORES
        route.append((i, base + (chip + hop) % CHIPS * CORES + core))
    return route


def pair_route(count):
    return [(i, i ^ 1) for i in range(count)]


def chip_route(count, k):
    return [(i, i ^ (CORES * k)) for i in range(count)]


def home_route(sections, count, hop):
    return [
        (s * count + i, (s + 1) % sections * count + j)
        for s in range(sections)
        for i, j in lane_route(count, hop)
    ]


def mm(a, b, dims=((1,), (0,))):
    return lax.dot_general(a, b, (dims, ((), ())), preferred_element_type=F32)


def halves(a):
    high = a.astype(BF16)
    return high, (a - high.astype(F32)).astype(BF16)


def mm3(a, b):
    (ah, al), (bh, bl) = a, b
    return mm(ah, bh) + (mm(ah, bl) + mm(al, bh))


def place_iota():
    row = lax.broadcasted_iota(jnp.int32, (BLOCK, BLOCK), 0)
    col = lax.broadcasted_iota(jnp.int32, (BLOCK, BLOCK), 1)
    return row, col


def lower_inverse(negs):
    row, col = place_iota()
    eye = jnp.where(row == col, 1.0, 0.0).astype(F32)
    small = 16
    near = row // small == col // small
    diag = [jnp.where(near, n, 0.0) for n in negs]
    total = [eye + d for d in diag]
    power = [d.astype(BF16) for d in diag]
    for _ in range((small - 1).bit_length() - 1):
        power = [mm(p, p).astype(BF16) for p in power]
        total = [t + mm(t.astype(BF16), p) for t, p in zip(total, power)]
    size = small
    while size < BLOCK:
        off = (row // (2 * size) == col // (2 * size)) & (row // size != col // size)
        cross = [jnp.where(off, n, 0.0).astype(BF16) for n in negs]
        short = [t.astype(BF16) for t in total]
        left = [mm(t, c).astype(BF16) for t, c in zip(short, cross)]
        total = [t + mm(m, s) for t, m, s in zip(total, left, short)]
        size *= 2
    return total


def unit(v):
    return v * lax.rsqrt(jnp.sum(v * v, axis=-1, keepdims=True) + 1e-06)


def attach_kernel(x_ref, decay_ref, out_ref, x_scr, decay_scr, sem):
    copies = [
        pltpu.make_async_copy(x_ref, x_scr, sem.at[0]),
        pltpu.make_async_copy(decay_ref, decay_scr, sem.at[1]),
    ]
    for copy in copies:
        copy.start()
    for copy in copies:
        copy.wait()
    columns = x_ref.shape[1] // BLOCK
    for c in range(columns):
        out_ref[c * BLOCK : (c + 1) * BLOCK, :] = x_scr[:, c * BLOCK : (c + 1) * BLOCK]
    rest = decay_scr[...]
    parts = []
    for _ in range(PARTS):
        parts.append(rest.astype(BF16).astype(F32))
        rest = rest - parts[-1]
    parts.append(jnp.zeros((EXTRA - PARTS * rest.shape[0], BLOCK), F32))
    out_ref[columns * BLOCK :, :] = jnp.concatenate(parts, axis=0).astype(BF16)


def attach(x, decay):
    hbm = pl.BlockSpec(memory_space=pltpu.HBM)
    return pl.pallas_call(
        attach_kernel,
        out_shape=jax.ShapeDtypeStruct((x.size // BLOCK + EXTRA, BLOCK), BF16),
        in_specs=[hbm, hbm],
        out_specs=pl.BlockSpec(memory_space=pltpu.VMEM),
        scratch_shapes=[
            pltpu.VMEM(x.shape, BF16),
            pltpu.VMEM(decay.shape, F32),
            pltpu.SemaphoreType.DMA((2,)),
        ],
        compiler_params=pltpu.CompilerParams(vmem_limit_bytes=VMEM_LIMIT),
        name="attach_decay",
    )(x, decay)


def rows_of(ref):
    columns = ref.shape[0] // BLOCK
    return jnp.concatenate([ref[c * BLOCK : (c + 1) * BLOCK, :] for c in range(columns)], axis=1)


def running_decay(parts, head, heads):
    row, col = place_iota()
    upto = jnp.where(row <= col, 1.0, 0.0).astype(BF16)
    line = lax.broadcasted_iota(jnp.int32, parts.shape, 0)
    mine = jnp.where((line % heads == head) & (line < PARTS * heads), parts.astype(F32), 0.0)
    return jnp.sum(mm(mine.astype(BF16), upto), axis=0, keepdims=True)


def block_terms(projs, cums):
    row, col = place_iota()
    hd = BLOCK
    q = [unit(p[:, :hd].astype(BF16).astype(F32)) for p in projs]
    k = [unit(p[:, hd : 2 * hd].astype(BF16).astype(F32)) for p in projs]
    v = [p[:, 2 * hd : 3 * hd].astype(BF16).astype(F32) for p in projs]
    beta = [jax.nn.sigmoid(p[:, 3 * hd :]) for p in projs]
    across = [jnp.broadcast_to(c, (BLOCK, BLOCK)) for c in cums]
    down = [jnp.transpose(a) for a in across]
    kb = [a.astype(BF16) for a in k]
    inner = [
        mm(jnp.concatenate([a.astype(BF16), b], axis=0), b, ((1,), (1,))) for a, b in zip(q, kb)
    ]
    ratio = [
        jnp.where(row >= col, jnp.exp(jnp.where(row >= col, d - a, 0.0)), 0.0)
        for d, a in zip(down, across)
    ]
    negs = [
        jnp.where(row > col, -(b * r * i[BLOCK:]), 0.0) for b, r, i in zip(beta, ratio, inner)
    ]
    growth = [jnp.exp(d) for d in down]
    rhs = [
        jnp.concatenate([b * g * a, b * c], axis=1) for b, g, a, c in zip(beta, growth, k, v)
    ]
    inv = lower_inverse(negs)
    solved = [mm(t.astype(BF16), r.astype(BF16)).astype(BF16) for t, r in zip(inv, rhs)]
    scores = [(i[:BLOCK] * r).astype(BF16) for i, r in zip(inner, ratio)]
    inside = [mm(s, w) for s, w in zip(scores, solved)]
    last = [d[BLOCK - 1 :, :] for d in down]
    tail = [(jnp.exp(e - d) * a).astype(BF16) for e, d, a in zip(last, down, k)]
    step = [mm(w, t, ((0,), (0,))) for w, t in zip(solved, tail)]
    fade = [jnp.exp(e) for e in last]
    reads = [g * a - i[:, :hd] for g, a, i in zip(growth, q, inside)]
    local = [i[:, hd:] for i in inside]
    return reads, local, step, fade


def where_am_i():
    place = lax.axis_index("seq")
    inner = jnp.bitwise_and(place, EXPERTS - 1)
    return place - inner, inner // CORES, jnp.bitwise_and(inner, 1)


def routes(kinds_ref, base):
    kinds = [kinds_ref[base + b] for b in range(EXPERTS)]
    ranks = []
    for b in range(EXPERTS):
        rank = jnp.int32(0)
        for earlier in range(b):
            rank = rank + jnp.where(kinds[earlier] == kinds[b], 1, 0)
        ranks.append(rank)
    return kinds, ranks


def sources(kinds, ranks, kind):
    found = []
    for slot in range(CAP):
        block = jnp.int32(0)
        for b in range(EXPERTS):
            block = block + jnp.where((kinds[b] == kind) & (ranks[b] == slot), b, 0)
        found.append(block)
    return found


def arrivals(chip, core):
    return [
        jnp.bitwise_and(chip + hop, CHIPS - 1) * CORES + (core if side == 0 else 1 - core)
        for hop in (0, 3, 1, 2)
        for side in (0, 1)
    ]


def normed(x, gain):
    xf = x.astype(F32)
    return (xf * lax.rsqrt(jnp.mean(xf * xf, axis=-1, keepdims=True) + 1e-06) * gain).astype(BF16)


def pair_terms(gain_ref, weight_ref, x_refs, norm_ref, put):
    _, chip, core = where_am_i()
    head = chip * CORES + core
    gain = gain_ref[...]
    columns = x_refs[0].shape[0] // BLOCK
    for j, ref in enumerate(x_refs):
        norm_ref[j * BLOCK : (j + 1) * BLOCK, :] = normed(rows_of(ref), gain)
    both = mm(norm_ref[...], weight_ref[...])
    reads, local, step, fade = block_terms(
        [both[:BLOCK], both[BLOCK:]],
        [running_decay(ref[columns * BLOCK :, :], head, columns) for ref in x_refs],
    )
    for i in range(len(x_refs)):
        put(i, reads[i].astype(BF16), local[i], step[i], jnp.broadcast_to(fade[i], (8, BLOCK)))


def term_scratch(count, width):
    return [pltpu.VMEM((count * BLOCK, width), BF16)]


def term_shapes(count):
    return (
        ((count, BLOCK, BLOCK), BF16),
        ((count, BLOCK, BLOCK), F32),
        ((count, 2 * BLOCK, BLOCK), F32),
        ((count, 8, BLOCK), F32),
    )


def terms_kernel(gain_ref, weight_ref, left_ref, right_ref, *refs):
    outs, scratch = refs[:4], refs[4:]

    def put(j, *values):
        for ref, value in zip(outs, values):
            ref[j] = value

    pair_terms(gain_ref, weight_ref, (left_ref, right_ref), *scratch, put)


def terms(gain, weight, blocks):
    count = len(blocks)
    width = gain.shape[1]
    vmem = pl.BlockSpec(memory_space=pltpu.VMEM)
    return pl.pallas_call(
        terms_kernel,
        out_shape=tuple(jax.ShapeDtypeStruct(*s) for s in term_shapes(count)),
        in_specs=[vmem] * 4,
        out_specs=(vmem,) * 4,
        scratch_shapes=term_scratch(count, width),
        compiler_params=pltpu.CompilerParams(vmem_limit_bytes=VMEM_LIMIT),
        cost_estimate=pl.CostEstimate(
            flops=4 * 10**9, bytes_accessed=3 * 10**6, transcendentals=10**5
        ),
        name="chunk_terms",
    )(gain, weight, *blocks)


def mix_kernel(counts, late, kinds_ref, out_gain_ref, *refs):
    base, chip, core = where_am_i()
    blocks = arrivals(chip, core)
    groups = [refs[4 * g : 4 * g + 4] for g in range(len(counts))]
    refs = refs[4 * len(counts) :]
    if late:
        gain_ref, weight_ref, left_ref, right_ref = refs[:4]
        refs = refs[4:]
    else:
        start_ref, refs = refs[0], refs[1:]
    outs, refs = refs[:CHIPS], refs[CHIPS:]
    scr, on_scr, refs = refs[:4], refs[4], refs[5:]
    at = 0
    for group, count in zip(groups, counts):
        for j in range(count):
            for ref, keep in zip(group, scr):
                keep[blocks[at]] = ref[j]
            at += 1
    if late:

        def put(j, *values):
            for ref, value in zip(scr, values):
                ref[blocks[at + j]] = value

        pair_terms(gain_ref, weight_ref, (left_ref, right_ref), *refs, put)
    reads_scr, local_scr, step_scr, fade_scr = scr
    state = jnp.zeros((BLOCK, BLOCK), F32) if late else start_ref[...]
    out_gain = out_gain_ref[...]
    for b in range(EXPERTS):
        split = halves(state)
        move = step_scr[b]
        mixed = mm(reads_scr[b], split[0], ((1,), (1,))) + local_scr[b]
        on_scr[b] = normed(mixed, out_gain)
        if b + 1 < EXPERTS:
            erase = mm3(split, halves(move[:BLOCK]))
            state = fade_scr[b][0:1, :] * state - erase + move[BLOCK:]
    kinds, ranks = routes(kinds_ref, base)
    for k in range(CHIPS):
        there = jnp.bitwise_xor(chip, k)
        for side in range(CORES):
            found = sources(kinds, ranks, there * CORES + side)
            for slot in range(CAP):
                outs[k][side, slot] = on_scr[found[slot]]


def mix(kinds, out_gain, groups, start=None, late=()):
    counts = tuple(g[0].shape[0] for g in groups)
    vmem = pl.BlockSpec(memory_space=pltpu.VMEM)
    extra = list(late) if late else [start]
    operands = [kinds, out_gain] + [a for g in groups for a in g] + extra
    sent = jax.ShapeDtypeStruct((CORES, CAP, BLOCK, BLOCK), BF16)
    return pl.pallas_call(
        partial(mix_kernel, counts, bool(late)),
        out_shape=(sent,) * CHIPS,
        in_specs=[pl.BlockSpec(memory_space=pltpu.SMEM)] + [vmem] * (len(operands) - 1),
        out_specs=(vmem,) * CHIPS,
        scratch_shapes=[pltpu.VMEM(*s) for s in term_shapes(EXPERTS)]
        + [pltpu.VMEM((EXPERTS, BLOCK, BLOCK), BF16)]
        + (term_scratch(2, late[0].shape[1]) if late else []),
        compiler_params=pltpu.CompilerParams(vmem_limit_bytes=VMEM_LIMIT),
        cost_estimate=pl.CostEstimate(
            flops=3 * 10**10, bytes_accessed=4 * 10**6, transcendentals=10**5
        ),
        name="state_walk",
    )(*operands)


def home_kernel(kinds_ref, own_ref, other_ref, *outs):
    base, chip, core = where_am_i()
    kinds, ranks = routes(kinds_ref, base)
    for k in range(CHIPS):
        home = jnp.bitwise_and(chip + k, CHIPS - 1) * CORES + core
        kind, rank = jnp.int32(0), jnp.int32(0)
        for b in range(EXPERTS):
            kind = kind + jnp.where(home == b, kinds[b], 0)
            rank = rank + jnp.where(home == b, ranks[b], 0)
        here = kind // CORES == chip
        mine = jnp.bitwise_and(kind, 1) == core
        outs[k][...] = jnp.zeros_like(outs[k])
        for slot in range(CAP):
            rows = slice(slot * BLOCK, (slot + 1) * BLOCK)

            @pl.when(here & mine & (rank == slot))
            def _():
                outs[k][...] = own_ref[rows, :]

            @pl.when(here & jnp.logical_not(mine) & (rank == slot))
            def _():
                outs[k][...] = other_ref[rows, :]


def homeward(kinds, own, other):
    vmem = pl.BlockSpec(memory_space=pltpu.VMEM)
    rows, width = own.shape
    return pl.pallas_call(
        home_kernel,
        out_shape=(jax.ShapeDtypeStruct((rows // CAP, width), BF16),) * CHIPS,
        in_specs=[pl.BlockSpec(memory_space=pltpu.SMEM), vmem, vmem],
        out_specs=(vmem,) * CHIPS,
        compiler_params=pltpu.CompilerParams(vmem_limit_bytes=VMEM_LIMIT),
        name="homeward",
    )(kinds, own, other)


def project(kinds_ref, gain_ref, out_weight_ref, x_refs, on_refs, x_scr, on_scr, h_ref, hn_ref, sem):
    base, chip, core = where_am_i()
    kinds, ranks = routes(kinds_ref, base)
    found = sources(kinds, ranks, chip * CORES + core)
    for slot in range(CAP):
        for block, ref in zip(arrivals(chip, core), x_refs):

            @pl.when(block == found[slot])
            def _():
                rows = ref.at[pl.ds(0, x_scr.shape[1]), :]
                pltpu.make_async_copy(rows, x_scr.at[slot], sem.at[slot]).start()

    for k in range(CHIPS):
        there = jnp.bitwise_xor(chip, k)
        for side in range(CORES):
            head = there * CORES + (core if side == 0 else 1 - core)
            at = pl.ds(pl.multiple_of(head * BLOCK, BLOCK), BLOCK)
            got = on_refs[k * CORES + side]
            for slot in range(CAP):
                on_scr[slot * BLOCK : (slot + 1) * BLOCK, at] = got[core, slot]
    for slot in range(CAP):
        rows = slice(slot * BLOCK, (slot + 1) * BLOCK)
        added = mm(on_scr[rows, :], out_weight_ref[...])
        rows_of_x = x_refs[0].at[pl.ds(0, x_scr.shape[1]), :]
        pltpu.make_async_copy(rows_of_x, x_scr.at[slot], sem.at[slot]).wait()
        hidden = (rows_of(x_scr.at[slot]).astype(F32) + added).astype(BF16)
        h_ref[rows, :] = hidden
        hn_ref[rows, :] = normed(hidden, gain_ref[...])


def project_kernel(kinds_ref, gain_ref, out_weight_ref, *refs):
    x_refs, on_refs = refs[:EXPERTS], refs[EXPERTS : 2 * EXPERTS]
    h_ref, hn_ref, x_scr, on_scr, sem = refs[2 * EXPERTS :]
    project(kinds_ref, gain_ref, out_weight_ref, x_refs, on_refs, x_scr, on_scr, h_ref, hn_ref, sem)


def expert_kernel(tile, kinds_ref, gain_ref, out_weight_ref, *refs):
    x_refs, on_refs = refs[:EXPERTS], refs[EXPERTS : 2 * EXPERTS]
    gate_ref, up_ref, down_ref, out_ref = refs[2 * EXPERTS : 2 * EXPERTS + 4]
    x_scr, on_scr, h_scr, hn_scr, act_scr, sem = refs[2 * EXPERTS + 4 :]
    project(
        kinds_ref, gain_ref, out_weight_ref, x_refs, on_refs, x_scr, on_scr, h_scr, hn_scr, sem
    )
    rows = hn_scr[...]
    for at in range(0, gate_ref.shape[3], tile):
        part = slice(at, at + tile)
        gate = mm(rows, gate_ref[0, 0, :, part])
        up = mm(rows, up_ref[0, 0, :, part])
        act_scr[:, part] = (gate / (1.0 + jnp.exp(-gate)) * up).astype(BF16)
    width = out_ref.shape[1]
    for at in range(0, width, width // 2):
        part = slice(at, at + width // 2)
        ffn = mm(act_scr[...], down_ref[0, 0, :, part]).astype(BF16).astype(F32)
        out_ref[:, part] = (h_scr[:, part].astype(F32) + ffn).astype(BF16)


def expert(kinds, gain, out_weight, blocks, ons, gate, up, down):
    rows, width = CAP * BLOCK, gain.shape[1]
    vmem = pl.BlockSpec(memory_space=pltpu.VMEM)
    return pl.pallas_call(
        partial(expert_kernel, min(512, gate.shape[3])),
        out_shape=jax.ShapeDtypeStruct((rows, width), BF16),
        in_specs=[pl.BlockSpec(memory_space=pltpu.SMEM), vmem, vmem]
        + [pl.BlockSpec(memory_space=pl.ANY)] * EXPERTS
        + [vmem] * (EXPERTS + 3),
        out_specs=vmem,
        scratch_shapes=[
            pltpu.VMEM((CAP, width, BLOCK), BF16),
            pltpu.VMEM((rows, width), BF16),
            pltpu.VMEM((rows, width), BF16),
            pltpu.VMEM((rows, width), BF16),
            pltpu.VMEM((rows, gate.shape[3]), BF16),
            pltpu.SemaphoreType.DMA((CAP,)),
        ],
        compiler_params=pltpu.CompilerParams(vmem_limit_bytes=VMEM_LIMIT),
        name="expert",
    )(kinds, gain, out_weight, *blocks, *ons, gate, up, down)


def project_only(kinds, gain, out_weight, blocks, ons):
    rows, width = CAP * BLOCK, gain.shape[1]
    vmem = pl.BlockSpec(memory_space=pltpu.VMEM)
    return pl.pallas_call(
        project_kernel,
        out_shape=(jax.ShapeDtypeStruct((rows, width), BF16),) * 2,
        in_specs=[pl.BlockSpec(memory_space=pltpu.SMEM), vmem, vmem]
        + [pl.BlockSpec(memory_space=pl.ANY)] * EXPERTS
        + [vmem] * EXPERTS,
        out_specs=(vmem, vmem),
        scratch_shapes=[
            pltpu.VMEM((CAP, width, BLOCK), BF16),
            pltpu.VMEM((rows, width), BF16),
            pltpu.SemaphoreType.DMA((CAP,)),
        ],
        compiler_params=pltpu.CompilerParams(vmem_limit_bytes=VMEM_LIMIT),
        name="project",
    )(kinds, gain, out_weight, *blocks, *ons)


def group_start(place, count, groups_of_terms):
    groups = count // EXPERTS
    ein = partial(jnp.einsum, precision=lax.Precision.HIGHEST)
    eye = jnp.eye(BLOCK, dtype=F32)
    step = jnp.concatenate([g[2] for g in groups_of_terms], axis=0)
    fade = jnp.concatenate([g[3] for g in groups_of_terms], axis=0)
    inner = place % EXPERTS
    order = jnp.argsort(jnp.stack(arrivals(inner // CORES, inner % CORES)))
    step, fade = jnp.take(step, order, axis=0), jnp.take(fade, order, axis=0)
    moves = fade[:, 0, :][:, None, :] * eye - step[:, :BLOCK]
    adds = step[:, BLOCK:]
    total, added = moves[0], adds[0]
    for b in range(1, EXPERTS):
        total, added = ein("ij,jk->ik", total, moves[b]), ein("vk,kj->vj", added, moves[b]) + adds[b]
    peers = [[g * EXPERTS + e for g in range(groups)] for e in range(EXPERTS)]
    gather = partial(lax.all_gather, axis_name="seq", axis_index_groups=peers)
    totals, addeds = gather(total), gather(added)

    def one(hop, state):
        return ein(
            "vk,kj->vj", state, lax.dynamic_index_in_dim(totals, hop, 0, False)
        ) + lax.dynamic_index_in_dim(addeds, hop, 0, False)

    return lax.fori_loop(0, place // EXPERTS, one, jnp.zeros((BLOCK, BLOCK), F32))


def per_device(
    held,
    log_decay,
    route_ids,
    norm_gain,
    qkv_weight,
    beta_weight,
    out_gain,
    out_weight,
    ffn_gain,
    gate_weight,
    up_weight,
    down_weight,
):
    count = lax.axis_size("seq")
    sections = lax.axis_size("segment")
    groups = count // EXPERTS
    place = lax.axis_index("seq")
    inner = place % EXPERTS
    width = held.shape[2]
    pair = partial(lax.ppermute, axis_name="seq", perm=pair_route(count))
    kinds = route_ids.reshape(-1)

    def hop(block, by):
        return lax.ppermute(block, "seq", lane_route(count, by))

    own = attach(held[0], log_decay[0].T)
    left = hop(own, 1)
    own_other = pair(own)
    later, _ = lax.optimization_barrier((own, own_other))
    right = hop(later, -1)

    def head_columns(at):
        return lax.dynamic_slice_in_dim(qkv_weight[0], at * width + inner * BLOCK, BLOCK, 1)

    beta_column = lax.dynamic_slice_in_dim(beta_weight[0], inner, 1, 1)
    weight = jnp.concatenate(
        [head_columns(0), head_columns(1), head_columns(2)]
        + [jnp.broadcast_to(beta_column, (width, BLOCK))],
        axis=1,
    )

    known = [terms(norm_gain, weight, (own, own_other))]
    left, _ = lax.optimization_barrier((left, known[0][0]))
    far = hop(left, 1)
    near = [(own, own_other), (left, pair(left))]
    known.append(terms(norm_gain, weight, near[1]))
    near.append((right, pair(right)))
    known.append(terms(norm_gain, weight, near[2]))
    far, *_ = lax.optimization_barrier((far, known[1][0], known[2][0]))
    last = (far, pair(far))
    if groups > 1:
        known.append(terms(norm_gain, weight, last))
        sends = mix(kinds, out_gain, known, start=group_start(place, count, known))
    else:
        sends = mix(kinds, out_gain, known, late=(norm_gain, weight, *last))

    got = [sends[0]] + [lax.ppermute(sends[k], "seq", chip_route(count, k)) for k in range(1, CHIPS)]
    ons = []
    for block in got:
        ons += [block, pair(block)]
    blocks = [block for two in near + [last] for block in two]

    if groups == 1:
        finished = expert(
            kinds, ffn_gain, out_weight[0], blocks, ons, gate_weight, up_weight, down_weight
        )
    else:
        hidden, hn = project_only(kinds, ffn_gain, out_weight[0], blocks, ons)
        peers = [[g * EXPERTS + e for g in range(groups)] for e in range(EXPERTS)]
        rows = lax.all_gather(hn, "seq", axis_index_groups=peers, tiled=True)
        gate = jnp.dot(rows, gate_weight[0, 0], preferred_element_type=F32)
        up = jnp.dot(rows, up_weight[0, 0], preferred_element_type=F32)
        act = (jax.nn.silu(gate) * up).astype(BF16)
        part = jnp.dot(act, down_weight[0, 0], preferred_element_type=F32)
        ffn = lax.psum_scatter(
            part, "seq", scatter_dimension=0, axis_index_groups=peers, tiled=True
        ).astype(BF16)
        finished = (hidden.astype(F32) + ffn.astype(F32)).astype(BF16)

    def send_home(block, by):
        return lax.ppermute(block, ("segment", "seq"), home_route(sections, count, by))

    here, right_home, far_home, left_home = homeward(kinds, finished, pair(finished))
    passed = hop(far_home, 1)
    from_right = send_home(left_home, -1)
    from_here = send_home(here, 0)
    from_left = send_home(passed + right_home, 1)
    return (from_left + from_right + from_here)[None]


def solution(mesh):
    placed = (
        P("segment", "seq", None),
        P("segment", "seq", None),
        P("segment", None, None),
        P("segment", None),
        P("segment", None, None),
        P("segment", None, None),
        P("segment", None),
        P("segment", None, None),
        P("segment", None),
        P("segment", "seq", None, None),
        P("segment", "seq", None, None),
        P("segment", "seq", None, None),
    )
    return jax.shard_map(
        per_device, mesh=mesh, in_specs=placed, out_specs=P("segment", "seq", None), check_vma=False
    )
```

```python
from functools import partial

import jax
import jax.numpy as jnp
from jax import lax
from jax.experimental import pallas as pl
from jax.experimental.pallas import tpu as pltpu
from jax.sharding import PartitionSpec as P

EXPERTS = 8
BLOCK = 128
CHIPS = 4
CORES = 2
CAP = 2
PARTS = 3
HOPS = (0, 3, 1, 2)
EXTRA = 32
F32 = jnp.float32
BF16 = jnp.bfloat16
VMEM_LIMIT = 16 * 1024 * 1024


def lane_route(count, hop):
    route = []
    for i in range(count):
        base, chip, core = i - i % EXPERTS, i % EXPERTS // CORES, i % CORES
        route.append((i, base + (chip + hop) % CHIPS * CORES + core))
    return route


def pair_route(count):
    return [(i, i ^ 1) for i in range(count)]


def chip_route(count, k):
    return [(i, i ^ (CORES * k)) for i in range(count)]


def home_route(sections, count, hop):
    return [
        (s * count + i, (s + 1) % sections * count + j)
        for s in range(sections)
        for i, j in lane_route(count, hop)
    ]


def mm(a, b, dims=((1,), (0,))):
    return lax.dot_general(a, b, (dims, ((), ())), preferred_element_type=F32)


def halves(a):
    high = a.astype(BF16)
    return high, (a - high.astype(F32)).astype(BF16)


def mm3(a, b):
    (ah, al), (bh, bl) = a, b
    return mm(ah, bh) + (mm(ah, bl) + mm(al, bh))


def place_iota():
    row = lax.broadcasted_iota(jnp.int32, (BLOCK, BLOCK), 0)
    col = lax.broadcasted_iota(jnp.int32, (BLOCK, BLOCK), 1)
    return row, col


def lower_inverse(negs):
    row, col = place_iota()
    eye = jnp.where(row == col, 1.0, 0.0).astype(F32)
    small = 16
    near = row // small == col // small
    diag = [jnp.where(near, n, 0.0) for n in negs]
    total = [eye + d for d in diag]
    power = [d.astype(BF16) for d in diag]
    for _ in range((small - 1).bit_length() - 1):
        power = [mm(p, p).astype(BF16) for p in power]
        total = [t + mm(t.astype(BF16), p) for t, p in zip(total, power)]
    size = small
    while size < BLOCK:
        off = (row // (2 * size) == col // (2 * size)) & (row // size != col // size)
        cross = [jnp.where(off, n, 0.0).astype(BF16) for n in negs]
        short = [t.astype(BF16) for t in total]
        left = [mm(t, c).astype(BF16) for t, c in zip(short, cross)]
        total = [t + mm(m, s) for t, m, s in zip(total, left, short)]
        size *= 2
    return total


def unit(v):
    return v * lax.rsqrt(jnp.sum(v * v, axis=-1, keepdims=True) + 1e-06)


def attach_kernel(x_ref, decay_ref, out_ref, x_scr, decay_scr, sem):
    copies = [
        pltpu.make_async_copy(x_ref, x_scr, sem.at[0]),
        pltpu.make_async_copy(decay_ref, decay_scr, sem.at[1]),
    ]
    for copy in copies:
        copy.start()
    for copy in copies:
        copy.wait()
    columns = x_ref.shape[1] // BLOCK
    for c in range(columns):
        out_ref[c * BLOCK : (c + 1) * BLOCK, :] = x_scr[:, c * BLOCK : (c + 1) * BLOCK]
    rest = decay_scr[...]
    parts = []
    for _ in range(PARTS):
        parts.append(rest.astype(BF16).astype(F32))
        rest = rest - parts[-1]
    parts.append(jnp.zeros((EXTRA - PARTS * rest.shape[0], BLOCK), F32))
    out_ref[columns * BLOCK :, :] = jnp.concatenate(parts, axis=0).astype(BF16)


def attach(x, decay):
    hbm = pl.BlockSpec(memory_space=pltpu.HBM)
    return pl.pallas_call(
        attach_kernel,
        out_shape=jax.ShapeDtypeStruct((x.size // BLOCK + EXTRA, BLOCK), BF16),
        in_specs=[hbm, hbm],
        out_specs=pl.BlockSpec(memory_space=pltpu.VMEM),
        scratch_shapes=[
            pltpu.VMEM(x.shape, BF16),
            pltpu.VMEM(decay.shape, F32),
            pltpu.SemaphoreType.DMA((2,)),
        ],
        compiler_params=pltpu.CompilerParams(vmem_limit_bytes=VMEM_LIMIT),
        name="attach_decay",
    )(x, decay)


def rows_of(ref):
    columns = ref.shape[0] // BLOCK
    return jnp.concatenate([ref[c * BLOCK : (c + 1) * BLOCK, :] for c in range(columns)], axis=1)


def running_decay(parts, head, heads):
    row, col = place_iota()
    upto = jnp.where(row <= col, 1.0, 0.0).astype(BF16)
    line = lax.broadcasted_iota(jnp.int32, parts.shape, 0)
    mine = jnp.where((line % heads == head) & (line < PARTS * heads), parts.astype(F32), 0.0)
    return jnp.sum(mm(mine.astype(BF16), upto), axis=0, keepdims=True)


def block_terms(projs, cums):
    row, col = place_iota()
    hd = BLOCK
    q = [unit(p[:, :hd].astype(BF16).astype(F32)) for p in projs]
    k = [unit(p[:, hd : 2 * hd].astype(BF16).astype(F32)) for p in projs]
    v = [p[:, 2 * hd : 3 * hd].astype(BF16).astype(F32) for p in projs]
    beta = [jax.nn.sigmoid(p[:, 3 * hd :]) for p in projs]
    across = [jnp.broadcast_to(c, (BLOCK, BLOCK)) for c in cums]
    down = [jnp.transpose(a) for a in across]
    kb = [a.astype(BF16) for a in k]
    inner = [
        mm(jnp.concatenate([a.astype(BF16), b], axis=0), b, ((1,), (1,))) for a, b in zip(q, kb)
    ]
    ratio = [
        jnp.where(row >= col, jnp.exp(jnp.where(row >= col, d - a, 0.0)), 0.0)
        for d, a in zip(down, across)
    ]
    negs = [
        jnp.where(row > col, -(b * r * i[BLOCK:]), 0.0) for b, r, i in zip(beta, ratio, inner)
    ]
    growth = [jnp.exp(d) for d in down]
    rhs = [
        jnp.concatenate([b * g * a, b * c], axis=1) for b, g, a, c in zip(beta, growth, k, v)
    ]
    inv = lower_inverse(negs)
    solved = [mm(t.astype(BF16), r.astype(BF16)).astype(BF16) for t, r in zip(inv, rhs)]
    scores = [(i[:BLOCK] * r).astype(BF16) for i, r in zip(inner, ratio)]
    inside = [mm(s, w) for s, w in zip(scores, solved)]
    last = [d[BLOCK - 1 :, :] for d in down]
    tail = [(jnp.exp(e - d) * a).astype(BF16) for e, d, a in zip(last, down, k)]
    step = [mm(w, t, ((0,), (0,))) for w, t in zip(solved, tail)]
    fade = [jnp.exp(e) for e in last]
    reads = [g * a - i[:, :hd] for g, a, i in zip(growth, q, inside)]
    local = [i[:, hd:] for i in inside]
    return reads, local, step, fade


def where_am_i():
    place = lax.axis_index("seq")
    inner = jnp.bitwise_and(place, EXPERTS - 1)
    return place - inner, inner // CORES, jnp.bitwise_and(inner, 1)


def routes(kinds_ref, base):
    kinds = [kinds_ref[base + b] for b in range(EXPERTS)]
    ranks = []
    for b in range(EXPERTS):
        rank = jnp.int32(0)
        for earlier in range(b):
            rank = rank + jnp.where(kinds[earlier] == kinds[b], 1, 0)
        ranks.append(rank)
    return kinds, ranks


def sources(kinds, ranks, kind):
    found = []
    for slot in range(CAP):
        block = jnp.int32(0)
        for b in range(EXPERTS):
            block = block + jnp.where((kinds[b] == kind) & (ranks[b] == slot), b, 0)
        found.append(block)
    return found


def arrivals(chip, core):
    return [
        jnp.bitwise_and(chip + hop, CHIPS - 1) * CORES + (core if side == 0 else 1 - core)
        for hop in HOPS
        for side in (0, 1)
    ]


def normed(x, gain):
    xf = x.astype(F32)
    return (xf * lax.rsqrt(jnp.mean(xf * xf, axis=-1, keepdims=True) + 1e-06) * gain).astype(BF16)


def pair_terms(gain_ref, weight_ref, x_refs, norm_ref, put):
    _, chip, core = where_am_i()
    head = chip * CORES + core
    gain = gain_ref[...]
    columns = x_refs[0].shape[0] // BLOCK
    for j, ref in enumerate(x_refs):
        norm_ref[j * BLOCK : (j + 1) * BLOCK, :] = normed(rows_of(ref), gain)
    both = mm(norm_ref[...], weight_ref[...])
    reads, local, step, fade = block_terms(
        [both[:BLOCK], both[BLOCK:]],
        [running_decay(ref[columns * BLOCK :, :], head, columns) for ref in x_refs],
    )
    for i, spot in ((0, core), (1, 1 - core)):
        put((0, 1), spot, reads[i].astype(BF16), local[i])
    ahead = core == 0
    step = [jnp.where(ahead, step[0], step[1]), jnp.where(ahead, step[1], step[0])]
    fade = [jnp.where(ahead, fade[0], fade[1]), jnp.where(ahead, fade[1], fade[0])]
    first, second = step
    cross = mm3(halves(first), halves(second[:BLOCK]))
    both_move = fade[1] * first[:BLOCK] + fade[0] * second[:BLOCK] - cross[:BLOCK]
    both_add = fade[1] * first[BLOCK:] - cross[BLOCK:] + second[BLOCK:]
    put((2, 3), 0, first, jnp.broadcast_to(fade[0], (8, BLOCK)))
    both_step = jnp.concatenate([both_move, both_add], axis=0)
    put((2, 3), 1, both_step, jnp.broadcast_to(fade[0] * fade[1], (8, BLOCK)))


def term_scratch(count, width):
    return [pltpu.VMEM((count * BLOCK, width), BF16)]


def term_shapes(count):
    return (
        ((count, BLOCK, BLOCK), BF16),
        ((count, BLOCK, BLOCK), F32),
        ((count, 2 * BLOCK, BLOCK), F32),
        ((count, 8, BLOCK), F32),
    )


def terms_kernel(gain_ref, weight_ref, left_ref, right_ref, *refs):
    outs, scratch = refs[:4], refs[4:]

    def put(which, spot, *values):
        for n, value in zip(which, values):
            outs[n][spot] = value

    pair_terms(gain_ref, weight_ref, (left_ref, right_ref), *scratch, put)


def terms(gain, weight, blocks):
    count = len(blocks)
    width = gain.shape[1]
    vmem = pl.BlockSpec(memory_space=pltpu.VMEM)
    return pl.pallas_call(
        terms_kernel,
        out_shape=tuple(jax.ShapeDtypeStruct(*s) for s in term_shapes(count)),
        in_specs=[vmem] * 4,
        out_specs=(vmem,) * 4,
        scratch_shapes=term_scratch(count, width),
        compiler_params=pltpu.CompilerParams(vmem_limit_bytes=VMEM_LIMIT),
        cost_estimate=pl.CostEstimate(
            flops=4 * 10**9, bytes_accessed=3 * 10**6, transcendentals=10**5
        ),
        name="chunk_terms",
    )(gain, weight, *blocks)


def mix_kernel(pairs, late, kinds_ref, out_gain_ref, *refs):
    base, chip, core = where_am_i()
    groups = [refs[4 * g : 4 * g + 4] for g in range(pairs)]
    refs = refs[4 * pairs :]
    if late:
        gain_ref, weight_ref, left_ref, right_ref = refs[:4]
        refs = refs[4:]
    else:
        start_ref, refs = refs[0], refs[1:]
    outs, refs = refs[:CHIPS], refs[CHIPS:]
    scr, on_scr, refs = refs[:4], refs[4], refs[5:]
    for group, hop in zip(groups, HOPS):
        spot = jnp.bitwise_and(chip + hop, CHIPS - 1) * CORES
        for ref, keep in zip(group, scr):
            for i in range(CORES):
                keep[spot + i] = ref[i]
    if late:
        late_spot = jnp.bitwise_and(chip + HOPS[-1], CHIPS - 1) * CORES

        def put(which, spot, *values):
            for n, value in zip(which, values):
                scr[n][late_spot + spot] = value

        pair_terms(gain_ref, weight_ref, (left_ref, right_ref), *refs, put)
    reads_scr, local_scr, step_scr, fade_scr = scr
    state = jnp.zeros((BLOCK, BLOCK), F32) if late else start_ref[...]
    out_gain = out_gain_ref[...]

    def after(split, state, at):
        move = step_scr[at]
        return fade_scr[at][0:1, :] * state - mm3(split, halves(move[:BLOCK])) + move[BLOCK:]

    for c in range(CHIPS):
        at = c * CORES
        split = halves(state)
        between = after(split, state, at)
        if c + 1 < CHIPS:
            state = after(split, state, at + 1)
        for b, before in ((at, split[0]), (at + 1, between.astype(BF16))):
            mixed = mm(reads_scr[b], before, ((1,), (1,))) + local_scr[b]
            on_scr[b] = normed(mixed, out_gain)
    kinds, ranks = routes(kinds_ref, base)
    for k in range(CHIPS):
        there = jnp.bitwise_xor(chip, k)
        for side in range(CORES):
            found = sources(kinds, ranks, there * CORES + side)
            for slot in range(CAP):
                outs[k][side, slot] = on_scr[found[slot]]


def mix(kinds, out_gain, groups, start=None, late=()):
    vmem = pl.BlockSpec(memory_space=pltpu.VMEM)
    extra = list(late) if late else [start]
    operands = [kinds, out_gain] + [a for g in groups for a in g] + extra
    sent = jax.ShapeDtypeStruct((CORES, CAP, BLOCK, BLOCK), BF16)
    return pl.pallas_call(
        partial(mix_kernel, len(groups), bool(late)),
        out_shape=(sent,) * CHIPS,
        in_specs=[pl.BlockSpec(memory_space=pltpu.SMEM)] + [vmem] * (len(operands) - 1),
        out_specs=(vmem,) * CHIPS,
        scratch_shapes=[pltpu.VMEM(*s) for s in term_shapes(EXPERTS)]
        + [pltpu.VMEM((EXPERTS, BLOCK, BLOCK), BF16)]
        + (term_scratch(2, late[0].shape[1]) if late else []),
        compiler_params=pltpu.CompilerParams(vmem_limit_bytes=VMEM_LIMIT),
        cost_estimate=pl.CostEstimate(
            flops=3 * 10**10, bytes_accessed=4 * 10**6, transcendentals=10**5
        ),
        name="state_walk",
    )(*operands)


def home_kernel(kinds_ref, own_ref, other_ref, *outs):
    base, chip, core = where_am_i()
    kinds, ranks = routes(kinds_ref, base)
    for k in range(CHIPS):
        home = jnp.bitwise_and(chip + k, CHIPS - 1) * CORES + core
        kind, rank = jnp.int32(0), jnp.int32(0)
        for b in range(EXPERTS):
            kind = kind + jnp.where(home == b, kinds[b], 0)
            rank = rank + jnp.where(home == b, ranks[b], 0)
        here = kind // CORES == chip
        mine = jnp.bitwise_and(kind, 1) == core
        outs[k][...] = jnp.zeros_like(outs[k])
        for slot in range(CAP):
            rows = slice(slot * BLOCK, (slot + 1) * BLOCK)

            @pl.when(here & mine & (rank == slot))
            def _():
                outs[k][...] = own_ref[rows, :]

            @pl.when(here & jnp.logical_not(mine) & (rank == slot))
            def _():
                outs[k][...] = other_ref[rows, :]


def homeward(kinds, own, other):
    vmem = pl.BlockSpec(memory_space=pltpu.VMEM)
    rows, width = own.shape
    return pl.pallas_call(
        home_kernel,
        out_shape=(jax.ShapeDtypeStruct((rows // CAP, width), BF16),) * CHIPS,
        in_specs=[pl.BlockSpec(memory_space=pltpu.SMEM), vmem, vmem],
        out_specs=(vmem,) * CHIPS,
        compiler_params=pltpu.CompilerParams(vmem_limit_bytes=VMEM_LIMIT),
        name="homeward",
    )(kinds, own, other)


def add_heads(half, out_weight_ref, on_refs, on_scr):
    _, chip, core = where_am_i()
    for k in range(CHIPS // 2):
        there = jnp.bitwise_and(jnp.bitwise_xor(chip, k), 1)
        for side in range(CORES):
            head = there * CORES + (core if side == 0 else 1 - core)
            at = pl.ds(pl.multiple_of(head * BLOCK, BLOCK), BLOCK)
            for slot in range(CAP):
                on_scr[slot * BLOCK : (slot + 1) * BLOCK, at] = on_refs[k * CORES + side][core, slot]
    depth = on_scr.shape[1]
    part = jnp.bitwise_xor(chip // 2, half)
    rows = pl.ds(pl.multiple_of(part * depth, depth), depth)
    return mm(on_scr[...], out_weight_ref[rows, :])


def early_kernel(kinds_ref, out_weight_ref, *refs):
    x_refs, on_refs = refs[:EXPERTS], refs[EXPERTS : EXPERTS + CHIPS]
    out_ref, x_scr, on_scr, sem = refs[EXPERTS + CHIPS :]
    base, chip, core = where_am_i()
    kinds, ranks = routes(kinds_ref, base)
    found = sources(kinds, ranks, chip * CORES + core)
    size = x_scr.shape[1]
    for slot in range(CAP):
        for block, ref in zip(arrivals(chip, core), x_refs):

            @pl.when(block == found[slot])
            def _():
                rows = ref.at[pl.ds(0, size), :]
                pltpu.make_async_copy(rows, x_scr.at[slot], sem.at[slot]).start()

    added = add_heads(0, out_weight_ref, on_refs, on_scr)
    for slot in range(CAP):
        rows = slice(slot * BLOCK, (slot + 1) * BLOCK)
        pltpu.make_async_copy(x_refs[0].at[pl.ds(0, size), :], x_scr.at[slot], sem.at[slot]).wait()
        out_ref[rows, :] = rows_of(x_scr.at[slot]).astype(F32) + added[rows]


def early_project(kinds, out_weight, blocks, ons):
    rows, width = CAP * BLOCK, out_weight.shape[1]
    vmem = pl.BlockSpec(memory_space=pltpu.VMEM)
    return pl.pallas_call(
        early_kernel,
        out_shape=jax.ShapeDtypeStruct((rows, width), F32),
        in_specs=[pl.BlockSpec(memory_space=pltpu.SMEM), vmem]
        + [pl.BlockSpec(memory_space=pl.ANY)] * EXPERTS
        + [vmem] * len(ons),
        out_specs=vmem,
        scratch_shapes=[
            pltpu.VMEM((CAP, width, BLOCK), BF16),
            pltpu.VMEM((rows, width // 2), BF16),
            pltpu.SemaphoreType.DMA((CAP,)),
        ],
        compiler_params=pltpu.CompilerParams(vmem_limit_bytes=VMEM_LIMIT),
        cost_estimate=pl.CostEstimate(flops=0, bytes_accessed=0, transcendentals=0),
        name="early_project",
    )(kinds, out_weight, *blocks, *ons)


def project(gain_ref, out_weight_ref, early_ref, on_refs, on_scr, h_ref, hn_ref):
    hidden = (early_ref[...] + add_heads(1, out_weight_ref, on_refs, on_scr)).astype(BF16)
    h_ref[...] = hidden
    hn_ref[...] = normed(hidden, gain_ref[...])


def project_kernel(gain_ref, out_weight_ref, early_ref, *refs):
    h_ref, hn_ref, on_scr = refs[CHIPS:]
    project(gain_ref, out_weight_ref, early_ref, refs[:CHIPS], on_scr, h_ref, hn_ref)


def expert_kernel(tile, gain_ref, out_weight_ref, early_ref, *refs):
    on_refs = refs[:CHIPS]
    gate_ref, up_ref, down_ref, out_ref = refs[CHIPS : CHIPS + 4]
    on_scr, h_scr, hn_scr, act_scr = refs[CHIPS + 4 :]
    project(gain_ref, out_weight_ref, early_ref, on_refs, on_scr, h_scr, hn_scr)
    rows = hn_scr[...]
    for at in range(0, gate_ref.shape[3], tile):
        part = slice(at, at + tile)
        gate = mm(rows, gate_ref[0, 0, :, part])
        up = mm(rows, up_ref[0, 0, :, part])
        act_scr[:, part] = (gate / (1.0 + jnp.exp(-gate)) * up).astype(BF16)
    width = out_ref.shape[1]
    for at in range(0, width, width // 2):
        part = slice(at, at + width // 2)
        ffn = mm(act_scr[...], down_ref[0, 0, :, part]).astype(BF16).astype(F32)
        out_ref[:, part] = (h_scr[:, part].astype(F32) + ffn).astype(BF16)


def expert(gain, out_weight, early, ons, gate, up, down):
    rows, width = early.shape
    vmem = pl.BlockSpec(memory_space=pltpu.VMEM)
    return pl.pallas_call(
        partial(expert_kernel, min(512, gate.shape[3])),
        out_shape=jax.ShapeDtypeStruct((rows, width), BF16),
        in_specs=[vmem] * (len(ons) + 6),
        out_specs=vmem,
        scratch_shapes=[
            pltpu.VMEM((rows, width // 2), BF16),
            pltpu.VMEM((rows, width), BF16),
            pltpu.VMEM((rows, width), BF16),
            pltpu.VMEM((rows, gate.shape[3]), BF16),
        ],
        compiler_params=pltpu.CompilerParams(vmem_limit_bytes=VMEM_LIMIT),
        name="expert",
    )(gain, out_weight, early, *ons, gate, up, down)


def project_only(gain, out_weight, early, ons):
    rows, width = early.shape
    vmem = pl.BlockSpec(memory_space=pltpu.VMEM)
    return pl.pallas_call(
        project_kernel,
        out_shape=(jax.ShapeDtypeStruct((rows, width), BF16),) * 2,
        in_specs=[vmem] * (len(ons) + 3),
        out_specs=(vmem, vmem),
        scratch_shapes=[pltpu.VMEM((rows, width // 2), BF16)],
        compiler_params=pltpu.CompilerParams(vmem_limit_bytes=VMEM_LIMIT),
        name="project",
    )(gain, out_weight, early, *ons)


def group_start(place, count, groups_of_terms):
    groups = count // EXPERTS
    ein = partial(jnp.einsum, precision=lax.Precision.HIGHEST)
    eye = jnp.eye(BLOCK, dtype=F32)
    step = jnp.stack([g[2][1] for g in groups_of_terms], axis=0)
    fade = jnp.stack([g[3][1] for g in groups_of_terms], axis=0)
    chip = place % EXPERTS // CORES
    order = jnp.argsort((chip + jnp.array(HOPS)) % CHIPS)
    step, fade = jnp.take(step, order, axis=0), jnp.take(fade, order, axis=0)
    moves = fade[:, 0, :][:, None, :] * eye - step[:, :BLOCK]
    adds = step[:, BLOCK:]
    total, added = moves[0], adds[0]
    for b in range(1, CHIPS):
        total, added = ein("ij,jk->ik", total, moves[b]), ein("vk,kj->vj", added, moves[b]) + adds[b]
    peers = [[g * EXPERTS + e for g in range(groups)] for e in range(EXPERTS)]
    gather = partial(lax.all_gather, axis_name="seq", axis_index_groups=peers)
    totals, addeds = gather(total), gather(added)

    def one(hop, state):
        return ein(
            "vk,kj->vj", state, lax.dynamic_index_in_dim(totals, hop, 0, False)
        ) + lax.dynamic_index_in_dim(addeds, hop, 0, False)

    return lax.fori_loop(0, place // EXPERTS, one, jnp.zeros((BLOCK, BLOCK), F32))


def per_device(
    held,
    log_decay,
    route_ids,
    norm_gain,
    qkv_weight,
    beta_weight,
    out_gain,
    out_weight,
    ffn_gain,
    gate_weight,
    up_weight,
    down_weight,
):
    count = lax.axis_size("seq")
    sections = lax.axis_size("segment")
    groups = count // EXPERTS
    place = lax.axis_index("seq")
    inner = place % EXPERTS
    width = held.shape[2]
    pair = partial(lax.ppermute, axis_name="seq", perm=pair_route(count))
    kinds = route_ids.reshape(-1)

    def hop(block, by):
        return lax.ppermute(block, "seq", lane_route(count, by))

    own = attach(held[0], log_decay[0].T)
    left = hop(own, 1)
    right = hop(own, -1)
    own_other = pair(own)

    def head_columns(at):
        return lax.dynamic_slice_in_dim(qkv_weight[0], at * width + inner * BLOCK, BLOCK, 1)

    beta_column = lax.dynamic_slice_in_dim(beta_weight[0], inner, 1, 1)
    weight = jnp.concatenate(
        [head_columns(0), head_columns(1), head_columns(2)]
        + [jnp.broadcast_to(beta_column, (width, BLOCK))],
        axis=1,
    )

    known = [terms(norm_gain, weight, (own, own_other))]
    right, _ = lax.optimization_barrier((right, known[0][0]))
    far = hop(right, -1)
    left, _ = lax.optimization_barrier((left, right))
    near = [(own, own_other), (left, pair(left))]
    known.append(terms(norm_gain, weight, near[1]))
    near.append((right, pair(right)))
    known.append(terms(norm_gain, weight, near[2]))
    far, *_ = lax.optimization_barrier((far, known[1][0], known[2][0]))
    last = (far, pair(far))
    if groups > 1:
        known.append(terms(norm_gain, weight, last))
        sends = mix(kinds, out_gain, known, start=group_start(place, count, known))
    else:
        sends = mix(kinds, out_gain, known, late=(norm_gain, weight, *last))

    got = [sends[0]] + [lax.ppermute(sends[k], "seq", chip_route(count, k)) for k in range(1, CHIPS)]
    blocks = [block for two in near + [last] for block in two]
    near_heads = [got[0], pair(got[0]), got[1], pair(got[1])]
    early = early_project(kinds, out_weight[0], blocks, near_heads)
    far_heads = [got[2], pair(got[2]), got[3], pair(got[3])]

    if groups == 1:
        finished = expert(
            ffn_gain, out_weight[0], early, far_heads, gate_weight, up_weight, down_weight
        )
    else:
        hidden, hn = project_only(ffn_gain, out_weight[0], early, far_heads)
        peers = [[g * EXPERTS + e for g in range(groups)] for e in range(EXPERTS)]
        rows = lax.all_gather(hn, "seq", axis_index_groups=peers, tiled=True)
        gate = jnp.dot(rows, gate_weight[0, 0], preferred_element_type=F32)
        up = jnp.dot(rows, up_weight[0, 0], preferred_element_type=F32)
        act = (jax.nn.silu(gate) * up).astype(BF16)
        part = jnp.dot(act, down_weight[0, 0], preferred_element_type=F32)
        ffn = lax.psum_scatter(
            part, "seq", scatter_dimension=0, axis_index_groups=peers, tiled=True
        ).astype(BF16)
        finished = (hidden.astype(F32) + ffn.astype(F32)).astype(BF16)

    def send_home(block, by):
        return lax.ppermute(block, ("segment", "seq"), home_route(sections, count, by))

    here, right_home, far_home, left_home = homeward(kinds, finished, pair(finished))
    passed = hop(far_home, 1)
    from_right = send_home(left_home, -1)
    from_here = send_home(here, 0)
    from_left = send_home(passed + right_home, 1)
    return (from_left + from_right + from_here)[None]


def solution(mesh):
    placed = (
        P("segment", "seq", None),
        P("segment", "seq", None),
        P("segment", None, None),
        P("segment", None),
        P("segment", None, None),
        P("segment", None, None),
        P("segment", None),
        P("segment", None, None),
        P("segment", None),
        P("segment", "seq", None, None),
        P("segment", "seq", None, None),
        P("segment", "seq", None, None),
    )
    return jax.shard_map(
        per_device, mesh=mesh, in_specs=placed, out_specs=P("segment", "seq", None), check_vma=False
    )
```

```python
from functools import partial

import jax
import jax.numpy as jnp
from jax import lax
from jax.experimental import pallas as pl
from jax.experimental.pallas import tpu as pltpu
from jax.sharding import PartitionSpec as P

EXPERTS = 8
BLOCK = 128
CHIPS = 4
CORES = 2
CAP = 2
PARTS = 3
HOPS = (0, 3, 1, 2)
EXTRA = 32
F32 = jnp.float32
BF16 = jnp.bfloat16
VMEM_LIMIT = 16 * 1024 * 1024


def lane_route(count, hop):
    route = []
    for i in range(count):
        base, chip, core = i - i % EXPERTS, i % EXPERTS // CORES, i % CORES
        route.append((i, base + (chip + hop) % CHIPS * CORES + core))
    return route


def pair_route(count):
    return [(i, i ^ 1) for i in range(count)]


def chip_route(count, k):
    return [(i, i ^ (CORES * k)) for i in range(count)]


def home_route(sections, count, hop):
    return [
        (s * count + i, (s + 1) % sections * count + j)
        for s in range(sections)
        for i, j in lane_route(count, hop)
    ]


def mm(a, b, dims=((1,), (0,))):
    return lax.dot_general(a, b, (dims, ((), ())), preferred_element_type=F32)


def halves(a):
    high = a.astype(BF16)
    return high, (a - high.astype(F32)).astype(BF16)


def mm3(a, b):
    (ah, al), (bh, bl) = a, b
    return mm(ah, bh) + (mm(ah, bl) + mm(al, bh))


def place_iota():
    row = lax.broadcasted_iota(jnp.int32, (BLOCK, BLOCK), 0)
    col = lax.broadcasted_iota(jnp.int32, (BLOCK, BLOCK), 1)
    return row, col


def lower_inverse(negs):
    row, col = place_iota()
    eye = jnp.where(row == col, 1.0, 0.0).astype(F32)
    small = 16
    near = row // small == col // small
    diag = [jnp.where(near, n, 0.0) for n in negs]
    total = [eye + d for d in diag]
    power = [d.astype(BF16) for d in diag]
    for _ in range((small - 1).bit_length() - 1):
        power = [mm(p, p).astype(BF16) for p in power]
        total = [t + mm(t.astype(BF16), p) for t, p in zip(total, power)]
    size = small
    while size < BLOCK:
        off = (row // (2 * size) == col // (2 * size)) & (row // size != col // size)
        cross = [jnp.where(off, n, 0.0).astype(BF16) for n in negs]
        short = [t.astype(BF16) for t in total]
        left = [mm(t, c).astype(BF16) for t, c in zip(short, cross)]
        total = [t + mm(m, s) for t, m, s in zip(total, left, short)]
        size *= 2
    return total


def unit(v):
    return v * lax.rsqrt(jnp.sum(v * v, axis=-1, keepdims=True) + 1e-06)


def attach_kernel(x_ref, decay_ref, out_ref, x_scr, decay_scr, sem):
    copies = [
        pltpu.make_async_copy(x_ref, x_scr, sem.at[0]),
        pltpu.make_async_copy(decay_ref, decay_scr, sem.at[1]),
    ]
    for copy in copies:
        copy.start()
    for copy in copies:
        copy.wait()
    columns = x_ref.shape[1] // BLOCK
    for c in range(columns):
        out_ref[c * BLOCK : (c + 1) * BLOCK, :] = x_scr[:, c * BLOCK : (c + 1) * BLOCK]
    rest = decay_scr[...]
    parts = []
    for _ in range(PARTS):
        parts.append(rest.astype(BF16).astype(F32))
        rest = rest - parts[-1]
    parts.append(jnp.zeros((EXTRA - PARTS * rest.shape[0], BLOCK), F32))
    out_ref[columns * BLOCK :, :] = jnp.concatenate(parts, axis=0).astype(BF16)


def attach(x, decay):
    hbm = pl.BlockSpec(memory_space=pltpu.HBM)
    return pl.pallas_call(
        attach_kernel,
        out_shape=jax.ShapeDtypeStruct((x.size // BLOCK + EXTRA, BLOCK), BF16),
        in_specs=[hbm, hbm],
        out_specs=pl.BlockSpec(memory_space=pltpu.VMEM),
        scratch_shapes=[
            pltpu.VMEM(x.shape, BF16),
            pltpu.VMEM(decay.shape, F32),
            pltpu.SemaphoreType.DMA((2,)),
        ],
        compiler_params=pltpu.CompilerParams(vmem_limit_bytes=VMEM_LIMIT),
        name="attach_decay",
    )(x, decay)


def rows_of(ref):
    columns = ref.shape[0] // BLOCK
    return jnp.concatenate([ref[c * BLOCK : (c + 1) * BLOCK, :] for c in range(columns)], axis=1)


def running_decay(parts, head, heads):
    row, col = place_iota()
    upto = jnp.where(row <= col, 1.0, 0.0).astype(BF16)
    line = lax.broadcasted_iota(jnp.int32, parts.shape, 0)
    mine = jnp.where((line % heads == head) & (line < PARTS * heads), parts.astype(F32), 0.0)
    return jnp.sum(mm(mine.astype(BF16), upto), axis=0, keepdims=True)


def block_terms(projs, cums):
    row, col = place_iota()
    hd = BLOCK
    q = [unit(p[:, :hd].astype(BF16).astype(F32)) for p in projs]
    k = [unit(p[:, hd : 2 * hd].astype(BF16).astype(F32)) for p in projs]
    v = [p[:, 2 * hd : 3 * hd].astype(BF16).astype(F32) for p in projs]
    beta = [jax.nn.sigmoid(p[:, 3 * hd :]) for p in projs]
    across = [jnp.broadcast_to(c, (BLOCK, BLOCK)) for c in cums]
    down = [jnp.transpose(a) for a in across]
    kb = [a.astype(BF16) for a in k]
    inner = [
        mm(jnp.concatenate([a.astype(BF16), b], axis=0), b, ((1,), (1,))) for a, b in zip(q, kb)
    ]
    ratio = [
        jnp.where(row >= col, jnp.exp(jnp.where(row >= col, d - a, 0.0)), 0.0)
        for d, a in zip(down, across)
    ]
    negs = [
        jnp.where(row > col, -(b * r * i[BLOCK:]), 0.0) for b, r, i in zip(beta, ratio, inner)
    ]
    growth = [jnp.exp(d) for d in down]
    rhs = [
        jnp.concatenate([b * g * a, b * c], axis=1) for b, g, a, c in zip(beta, growth, k, v)
    ]
    inv = lower_inverse(negs)
    solved = [mm(t.astype(BF16), r.astype(BF16)).astype(BF16) for t, r in zip(inv, rhs)]
    scores = [(i[:BLOCK] * r).astype(BF16) for i, r in zip(inner, ratio)]
    inside = [mm(s, w) for s, w in zip(scores, solved)]
    last = [d[BLOCK - 1 :, :] for d in down]
    tail = [(jnp.exp(e - d) * a).astype(BF16) for e, d, a in zip(last, down, k)]
    step = [mm(w, t, ((0,), (0,))) for w, t in zip(solved, tail)]
    fade = [jnp.exp(e) for e in last]
    reads = [g * a - i[:, :hd] for g, a, i in zip(growth, q, inside)]
    local = [i[:, hd:] for i in inside]
    return reads, local, step, fade


def where_am_i():
    place = lax.axis_index("seq")
    inner = jnp.bitwise_and(place, EXPERTS - 1)
    return place - inner, inner // CORES, jnp.bitwise_and(inner, 1)


def routes(kinds_ref, base):
    kinds = [kinds_ref[base + b] for b in range(EXPERTS)]
    ranks = []
    for b in range(EXPERTS):
        rank = jnp.int32(0)
        for earlier in range(b):
            rank = rank + jnp.where(kinds[earlier] == kinds[b], 1, 0)
        ranks.append(rank)
    return kinds, ranks


def sources(kinds, ranks, kind):
    found = []
    for slot in range(CAP):
        block = jnp.int32(0)
        for b in range(EXPERTS):
            block = block + jnp.where((kinds[b] == kind) & (ranks[b] == slot), b, 0)
        found.append(block)
    return found


def arrivals(chip, core):
    return [
        jnp.bitwise_and(chip + hop, CHIPS - 1) * CORES + (core if side == 0 else 1 - core)
        for hop in HOPS
        for side in (0, 1)
    ]


def normed(x, gain):
    xf = x.astype(F32)
    return (xf * lax.rsqrt(jnp.mean(xf * xf, axis=-1, keepdims=True) + 1e-06) * gain).astype(BF16)


def pair_terms(gain_ref, weight_ref, x_refs, norm_ref, put):
    _, chip, core = where_am_i()
    head = chip * CORES + core
    gain = gain_ref[...]
    columns = x_refs[0].shape[0] // BLOCK
    for j, ref in enumerate(x_refs):
        norm_ref[j * BLOCK : (j + 1) * BLOCK, :] = normed(rows_of(ref), gain)
    both = mm(norm_ref[...], weight_ref[...])
    reads, local, step, fade = block_terms(
        [both[:BLOCK], both[BLOCK:]],
        [running_decay(ref[columns * BLOCK :, :], head, columns) for ref in x_refs],
    )
    for i, spot in ((0, core), (1, 1 - core)):
        put((0, 1), spot, reads[i].astype(BF16), local[i])
    ahead = core == 0
    step = [jnp.where(ahead, step[0], step[1]), jnp.where(ahead, step[1], step[0])]
    fade = [jnp.where(ahead, fade[0], fade[1]), jnp.where(ahead, fade[1], fade[0])]
    first, second = step
    cross = mm3(halves(first), halves(second[:BLOCK]))
    both_move = fade[1] * first[:BLOCK] + fade[0] * second[:BLOCK] - cross[:BLOCK]
    both_add = fade[1] * first[BLOCK:] - cross[BLOCK:] + second[BLOCK:]
    put((2, 3), 0, first, jnp.broadcast_to(fade[0], (8, BLOCK)))
    both_step = jnp.concatenate([both_move, both_add], axis=0)
    put((2, 3), 1, both_step, jnp.broadcast_to(fade[0] * fade[1], (8, BLOCK)))


def term_scratch(count, width):
    return [pltpu.VMEM((count * BLOCK, width), BF16)]


def term_shapes(count):
    return (
        ((count, BLOCK, BLOCK), BF16),
        ((count, BLOCK, BLOCK), F32),
        ((count, 2 * BLOCK, BLOCK), F32),
        ((count, 8, BLOCK), F32),
    )


def terms_kernel(gain_ref, weight_ref, left_ref, right_ref, *refs):
    outs, scratch = refs[:4], refs[4:]

    def put(which, spot, *values):
        for n, value in zip(which, values):
            outs[n][spot] = value

    pair_terms(gain_ref, weight_ref, (left_ref, right_ref), *scratch, put)


def terms(gain, weight, blocks):
    count = len(blocks)
    width = gain.shape[1]
    vmem = pl.BlockSpec(memory_space=pltpu.VMEM)
    return pl.pallas_call(
        terms_kernel,
        out_shape=tuple(jax.ShapeDtypeStruct(*s) for s in term_shapes(count)),
        in_specs=[vmem] * 4,
        out_specs=(vmem,) * 4,
        scratch_shapes=term_scratch(count, width),
        compiler_params=pltpu.CompilerParams(vmem_limit_bytes=VMEM_LIMIT),
        cost_estimate=pl.CostEstimate(
            flops=4 * 10**9, bytes_accessed=3 * 10**6, transcendentals=10**5
        ),
        name="chunk_terms",
    )(gain, weight, *blocks)


def mix_kernel(pairs, late, kinds_ref, out_gain_ref, *refs):
    base, chip, core = where_am_i()
    groups = [refs[4 * g : 4 * g + 4] for g in range(pairs)]
    refs = refs[4 * pairs :]
    if late:
        gain_ref, weight_ref, left_ref, right_ref = refs[:4]
        refs = refs[4:]
    else:
        start_ref, refs = refs[0], refs[1:]
    outs, refs = refs[:CHIPS], refs[CHIPS:]
    scr, on_scr, refs = refs[:4], refs[4], refs[5:]
    for group, hop in zip(groups, HOPS):
        spot = jnp.bitwise_and(chip + hop, CHIPS - 1) * CORES
        for ref, keep in zip(group, scr):
            for i in range(CORES):
                keep[spot + i] = ref[i]
    if late:
        late_spot = jnp.bitwise_and(chip + HOPS[-1], CHIPS - 1) * CORES

        def put(which, spot, *values):
            for n, value in zip(which, values):
                scr[n][late_spot + spot] = value

        pair_terms(gain_ref, weight_ref, (left_ref, right_ref), *refs, put)
    reads_scr, local_scr, step_scr, fade_scr = scr
    state = jnp.zeros((BLOCK, BLOCK), F32) if late else start_ref[...]
    out_gain = out_gain_ref[...]

    def after(split, state, at):
        move = step_scr[at]
        return fade_scr[at][0:1, :] * state - mm3(split, halves(move[:BLOCK])) + move[BLOCK:]

    for c in range(CHIPS):
        at = c * CORES
        split = halves(state)
        between = after(split, state, at)
        if c + 1 < CHIPS:
            state = after(split, state, at + 1)
        for b, before in ((at, split[0]), (at + 1, between.astype(BF16))):
            mixed = mm(reads_scr[b], before, ((1,), (1,))) + local_scr[b]
            on_scr[b] = normed(mixed, out_gain)
    kinds, ranks = routes(kinds_ref, base)
    for k in range(CHIPS):
        there = jnp.bitwise_xor(chip, k)
        for side in range(CORES):
            found = sources(kinds, ranks, there * CORES + side)
            for slot in range(CAP):
                outs[k][side, slot] = on_scr[found[slot]]


def mix(kinds, out_gain, groups, start=None, late=()):
    vmem = pl.BlockSpec(memory_space=pltpu.VMEM)
    extra = list(late) if late else [start]
    operands = [kinds, out_gain] + [a for g in groups for a in g] + extra
    sent = jax.ShapeDtypeStruct((CORES, CAP, BLOCK, BLOCK), BF16)
    return pl.pallas_call(
        partial(mix_kernel, len(groups), bool(late)),
        out_shape=(sent,) * CHIPS,
        in_specs=[pl.BlockSpec(memory_space=pltpu.SMEM)] + [vmem] * (len(operands) - 1),
        out_specs=(vmem,) * CHIPS,
        scratch_shapes=[pltpu.VMEM(*s) for s in term_shapes(EXPERTS)]
        + [pltpu.VMEM((EXPERTS, BLOCK, BLOCK), BF16)]
        + (term_scratch(2, late[0].shape[1]) if late else []),
        compiler_params=pltpu.CompilerParams(vmem_limit_bytes=VMEM_LIMIT),
        cost_estimate=pl.CostEstimate(
            flops=3 * 10**10, bytes_accessed=4 * 10**6, transcendentals=10**5
        ),
        name="state_walk",
    )(*operands)


def home_kernel(kinds_ref, own_ref, other_ref, *outs):
    base, chip, core = where_am_i()
    kinds, ranks = routes(kinds_ref, base)
    for k in range(CHIPS):
        home = jnp.bitwise_and(chip + k, CHIPS - 1) * CORES + core
        kind, rank = jnp.int32(0), jnp.int32(0)
        for b in range(EXPERTS):
            kind = kind + jnp.where(home == b, kinds[b], 0)
            rank = rank + jnp.where(home == b, ranks[b], 0)
        here = kind // CORES == chip
        mine = jnp.bitwise_and(kind, 1) == core
        outs[k][...] = jnp.zeros_like(outs[k])
        for slot in range(CAP):
            rows = slice(slot * BLOCK, (slot + 1) * BLOCK)

            @pl.when(here & mine & (rank == slot))
            def _():
                outs[k][...] = own_ref[rows, :]

            @pl.when(here & jnp.logical_not(mine) & (rank == slot))
            def _():
                outs[k][...] = other_ref[rows, :]


def homeward(kinds, own, other):
    vmem = pl.BlockSpec(memory_space=pltpu.VMEM)
    rows, width = own.shape
    return pl.pallas_call(
        home_kernel,
        out_shape=(jax.ShapeDtypeStruct((rows // CAP, width), BF16),) * CHIPS,
        in_specs=[pl.BlockSpec(memory_space=pltpu.SMEM), vmem, vmem],
        out_specs=(vmem,) * CHIPS,
        compiler_params=pltpu.CompilerParams(vmem_limit_bytes=VMEM_LIMIT),
        name="homeward",
    )(kinds, own, other)


def add_heads(half, out_weight_ref, on_refs, on_scr):
    _, chip, core = where_am_i()
    for k in range(CHIPS // 2):
        there = jnp.bitwise_and(jnp.bitwise_xor(chip, k), 1)
        for side in range(CORES):
            head = there * CORES + (core if side == 0 else 1 - core)
            at = pl.ds(pl.multiple_of(head * BLOCK, BLOCK), BLOCK)
            for slot in range(CAP):
                on_scr[slot * BLOCK : (slot + 1) * BLOCK, at] = on_refs[k * CORES + side][core, slot]
    depth = on_scr.shape[1]
    part = jnp.bitwise_xor(chip // 2, half)
    rows = pl.ds(pl.multiple_of(part * depth, depth), depth)
    return mm(on_scr[...], out_weight_ref[rows, :])


def early_kernel(kinds_ref, out_weight_ref, *refs):
    x_refs, on_refs = refs[:EXPERTS], refs[EXPERTS : EXPERTS + CHIPS]
    out_ref, x_scr, on_scr, sem = refs[EXPERTS + CHIPS :]
    base, chip, core = where_am_i()
    kinds, ranks = routes(kinds_ref, base)
    found = sources(kinds, ranks, chip * CORES + core)
    size = x_scr.shape[1]
    for slot in range(CAP):
        for block, ref in zip(arrivals(chip, core), x_refs):

            @pl.when(block == found[slot])
            def _():
                rows = ref.at[pl.ds(0, size), :]
                pltpu.make_async_copy(rows, x_scr.at[slot], sem.at[slot]).start()

    added = add_heads(0, out_weight_ref, on_refs, on_scr)
    for slot in range(CAP):
        rows = slice(slot * BLOCK, (slot + 1) * BLOCK)
        pltpu.make_async_copy(x_refs[0].at[pl.ds(0, size), :], x_scr.at[slot], sem.at[slot]).wait()
        out_ref[rows, :] = rows_of(x_scr.at[slot]).astype(F32) + added[rows]


def early_project(kinds, out_weight, blocks, ons):
    rows, width = CAP * BLOCK, out_weight.shape[1]
    vmem = pl.BlockSpec(memory_space=pltpu.VMEM)
    return pl.pallas_call(
        early_kernel,
        out_shape=jax.ShapeDtypeStruct((rows, width), F32),
        in_specs=[pl.BlockSpec(memory_space=pltpu.SMEM), vmem]
        + [pl.BlockSpec(memory_space=pl.ANY)] * EXPERTS
        + [vmem] * len(ons),
        out_specs=vmem,
        scratch_shapes=[
            pltpu.VMEM((CAP, width, BLOCK), BF16),
            pltpu.VMEM((rows, width // 2), BF16),
            pltpu.SemaphoreType.DMA((CAP,)),
        ],
        compiler_params=pltpu.CompilerParams(vmem_limit_bytes=VMEM_LIMIT),
        cost_estimate=pl.CostEstimate(flops=0, bytes_accessed=0, transcendentals=0),
        name="early_project",
    )(kinds, out_weight, *blocks, *ons)


def project(gain_ref, out_weight_ref, early_ref, on_refs, on_scr, h_ref, hn_ref):
    hidden = (early_ref[...] + add_heads(1, out_weight_ref, on_refs, on_scr)).astype(BF16)
    h_ref[...] = hidden
    hn_ref[...] = normed(hidden, gain_ref[...])


def project_kernel(gain_ref, out_weight_ref, early_ref, *refs):
    h_ref, hn_ref, on_scr = refs[CHIPS:]
    project(gain_ref, out_weight_ref, early_ref, refs[:CHIPS], on_scr, h_ref, hn_ref)


def expert_kernel(tile, gain_ref, out_weight_ref, early_ref, *refs):
    on_refs = refs[:CHIPS]
    gate_ref, up_ref, down_ref, out_ref = refs[CHIPS : CHIPS + 4]
    on_scr, h_scr, hn_scr, act_scr = refs[CHIPS + 4 :]
    project(gain_ref, out_weight_ref, early_ref, on_refs, on_scr, h_scr, hn_scr)
    rows = hn_scr[...]
    for at in range(0, gate_ref.shape[3], tile):
        part = slice(at, at + tile)
        gate = mm(rows, gate_ref[0, 0, :, part])
        up = mm(rows, up_ref[0, 0, :, part])
        act_scr[:, part] = (gate / (1.0 + jnp.exp(-gate)) * up).astype(BF16)
    width = out_ref.shape[1]
    for at in range(0, width, width // 2):
        part = slice(at, at + width // 2)
        ffn = mm(act_scr[...], down_ref[0, 0, :, part]).astype(BF16).astype(F32)
        out_ref[:, part] = (h_scr[:, part].astype(F32) + ffn).astype(BF16)


def expert(gain, out_weight, early, ons, gate, up, down):
    rows, width = early.shape
    vmem = pl.BlockSpec(memory_space=pltpu.VMEM)
    return pl.pallas_call(
        partial(expert_kernel, min(512, gate.shape[3])),
        out_shape=jax.ShapeDtypeStruct((rows, width), BF16),
        in_specs=[vmem] * (len(ons) + 6),
        out_specs=vmem,
        scratch_shapes=[
            pltpu.VMEM((rows, width // 2), BF16),
            pltpu.VMEM((rows, width), BF16),
            pltpu.VMEM((rows, width), BF16),
            pltpu.VMEM((rows, gate.shape[3]), BF16),
        ],
        compiler_params=pltpu.CompilerParams(vmem_limit_bytes=VMEM_LIMIT),
        name="expert",
    )(gain, out_weight, early, *ons, gate, up, down)


def project_only(gain, out_weight, early, ons):
    rows, width = early.shape
    vmem = pl.BlockSpec(memory_space=pltpu.VMEM)
    return pl.pallas_call(
        project_kernel,
        out_shape=(jax.ShapeDtypeStruct((rows, width), BF16),) * 2,
        in_specs=[vmem] * (len(ons) + 3),
        out_specs=(vmem, vmem),
        scratch_shapes=[pltpu.VMEM((rows, width // 2), BF16)],
        compiler_params=pltpu.CompilerParams(vmem_limit_bytes=VMEM_LIMIT),
        name="project",
    )(gain, out_weight, early, *ons)


def group_start(place, count, groups_of_terms):
    groups = count // EXPERTS
    ein = partial(jnp.einsum, precision=lax.Precision.HIGHEST)
    eye = jnp.eye(BLOCK, dtype=F32)
    step = jnp.stack([g[2][1] for g in groups_of_terms], axis=0)
    fade = jnp.stack([g[3][1] for g in groups_of_terms], axis=0)
    chip = place % EXPERTS // CORES
    order = jnp.argsort((chip + jnp.array(HOPS)) % CHIPS)
    step, fade = jnp.take(step, order, axis=0), jnp.take(fade, order, axis=0)
    moves = fade[:, 0, :][:, None, :] * eye - step[:, :BLOCK]
    adds = step[:, BLOCK:]
    total, added = moves[0], adds[0]
    for b in range(1, CHIPS):
        total, added = ein("ij,jk->ik", total, moves[b]), ein("vk,kj->vj", added, moves[b]) + adds[b]
    peers = [[g * EXPERTS + e for g in range(groups)] for e in range(EXPERTS)]
    gather = partial(lax.all_gather, axis_name="seq", axis_index_groups=peers)
    totals, addeds = gather(total), gather(added)

    def one(hop, state):
        return ein(
            "vk,kj->vj", state, lax.dynamic_index_in_dim(totals, hop, 0, False)
        ) + lax.dynamic_index_in_dim(addeds, hop, 0, False)

    return lax.fori_loop(0, place // EXPERTS, one, jnp.zeros((BLOCK, BLOCK), F32))


def per_device(
    held,
    log_decay,
    route_ids,
    norm_gain,
    qkv_weight,
    beta_weight,
    out_gain,
    out_weight,
    ffn_gain,
    gate_weight,
    up_weight,
    down_weight,
):
    count = lax.axis_size("seq")
    sections = lax.axis_size("segment")
    groups = count // EXPERTS
    place = lax.axis_index("seq")
    inner = place % EXPERTS
    width = held.shape[2]
    pair = partial(lax.ppermute, axis_name="seq", perm=pair_route(count))
    kinds = route_ids.reshape(-1)

    def hop(block, by):
        return lax.ppermute(block, "seq", lane_route(count, by))

    own = attach(held[0], log_decay[0].T)
    left = hop(own, 1)
    right = hop(own, -1)
    own_other = pair(own)

    def head_columns(at):
        return lax.dynamic_slice_in_dim(qkv_weight[0], at * width + inner * BLOCK, BLOCK, 1)

    beta_column = lax.dynamic_slice_in_dim(beta_weight[0], inner, 1, 1)
    weight = jnp.concatenate(
        [head_columns(0), head_columns(1), head_columns(2)]
        + [jnp.broadcast_to(beta_column, (width, BLOCK))],
        axis=1,
    )

    known = [terms(norm_gain, weight, (own, own_other))]
    right, _ = lax.optimization_barrier((right, known[0][0]))
    far = hop(right, -1)
    left, _ = lax.optimization_barrier((left, right))
    near = [(own, own_other), (left, pair(left))]
    known.append(terms(norm_gain, weight, near[1]))
    near.append((right, pair(right)))
    known.append(terms(norm_gain, weight, near[2]))
    far, *_ = lax.optimization_barrier((far, known[1][0], known[2][0]))
    last = (far, pair(far))
    if groups > 1:
        known.append(terms(norm_gain, weight, last))
        sends = mix(kinds, out_gain, known, start=group_start(place, count, known))
    else:
        sends = mix(kinds, out_gain, known, late=(norm_gain, weight, *last))

    got = [sends[0]] + [lax.ppermute(sends[k], "seq", chip_route(count, k)) for k in range(1, CHIPS)]
    blocks = [block for two in near + [last] for block in two]
    near_heads = [got[0], pair(got[0]), got[1], pair(got[1])]
    early = early_project(kinds, out_weight[0], blocks, near_heads)
    far_heads = [got[2], pair(got[2]), got[3], pair(got[3])]

    if groups == 1:
        finished = expert(
            ffn_gain, out_weight[0], early, far_heads, gate_weight, up_weight, down_weight
        )
    else:
        hidden, hn = project_only(ffn_gain, out_weight[0], early, far_heads)
        peers = [[g * EXPERTS + e for g in range(groups)] for e in range(EXPERTS)]
        rows = lax.all_gather(hn, "seq", axis_index_groups=peers, tiled=True)
        gate = jnp.dot(rows, gate_weight[0, 0], preferred_element_type=F32)
        up = jnp.dot(rows, up_weight[0, 0], preferred_element_type=F32)
        act = (jax.nn.silu(gate) * up).astype(BF16)
        part = jnp.dot(act, down_weight[0, 0], preferred_element_type=F32)
        ffn = lax.psum_scatter(
            part, "seq", scatter_dimension=0, axis_index_groups=peers, tiled=True
        ).astype(BF16)
        finished = (hidden.astype(F32) + ffn.astype(F32)).astype(BF16)

    def send_home(block, by):
        return lax.ppermute(block, ("segment", "seq"), home_route(sections, count, by))

    here, right_home, far_home, left_home = homeward(kinds, finished, pair(finished))
    passed = hop(far_home, -1)
    from_right = send_home(right_home, 1)
    from_here = send_home(here, 0)
    from_left = send_home(passed + left_home, -1)
    return (from_left + from_right + from_here)[None]


def solution(mesh):
    placed = (
        P("segment", "seq", None),
        P("segment", "seq", None),
        P("segment", None, None),
        P("segment", None),
        P("segment", None, None),
        P("segment", None, None),
        P("segment", None),
        P("segment", None, None),
        P("segment", None),
        P("segment", "seq", None, None),
        P("segment", "seq", None, None),
        P("segment", "seq", None, None),
    )
    return jax.shard_map(
        per_device, mesh=mesh, in_specs=placed, out_specs=P("segment", "seq", None), check_vma=False
    )
```

```python
from functools import partial

import jax
import jax.numpy as jnp
from jax import lax
from jax.experimental import pallas as pl
from jax.experimental.pallas import tpu as pltpu
from jax.sharding import PartitionSpec as P

EXPERTS = 8
BLOCK = 128
CHIPS = 4
CORES = 2
CAP = 2
PARTS = 3
HOPS = (0, 3, 1, 2)
EXTRA = 32
F32 = jnp.float32
BF16 = jnp.bfloat16
VMEM_LIMIT = 16 * 1024 * 1024


def lane_route(count, hop):
    route = []
    for i in range(count):
        base, chip, core = i - i % EXPERTS, i % EXPERTS // CORES, i % CORES
        route.append((i, base + (chip + hop) % CHIPS * CORES + core))
    return route


def pair_route(count):
    return [(i, i ^ 1) for i in range(count)]


def chip_route(count, k):
    return [(i, i ^ (CORES * k)) for i in range(count)]


def home_route(sections, count, hop):
    return [
        (s * count + i, (s + 1) % sections * count + j)
        for s in range(sections)
        for i, j in lane_route(count, hop)
    ]


def mm(a, b, dims=((1,), (0,))):
    return lax.dot_general(a, b, (dims, ((), ())), preferred_element_type=F32)


def halves(a):
    high = a.astype(BF16)
    return high, (a - high.astype(F32)).astype(BF16)


def mm3(a, b):
    (ah, al), (bh, bl) = a, b
    return mm(ah, bh) + (mm(ah, bl) + mm(al, bh))


def place_iota():
    row = lax.broadcasted_iota(jnp.int32, (BLOCK, BLOCK), 0)
    col = lax.broadcasted_iota(jnp.int32, (BLOCK, BLOCK), 1)
    return row, col


def lower_inverse(negs):
    row, col = place_iota()
    eye = jnp.where(row == col, 1.0, 0.0).astype(F32)
    small = 16
    near = row // small == col // small
    diag = [jnp.where(near, n, 0.0) for n in negs]
    total = [eye + d for d in diag]
    power = [d.astype(BF16) for d in diag]
    for _ in range((small - 1).bit_length() - 1):
        power = [mm(p, p).astype(BF16) for p in power]
        total = [t + mm(t.astype(BF16), p) for t, p in zip(total, power)]
    size = small
    while size < BLOCK:
        off = (row // (2 * size) == col // (2 * size)) & (row // size != col // size)
        cross = [jnp.where(off, n, 0.0).astype(BF16) for n in negs]
        short = [t.astype(BF16) for t in total]
        left = [mm(t, c).astype(BF16) for t, c in zip(short, cross)]
        total = [t + mm(m, s) for t, m, s in zip(total, left, short)]
        size *= 2
    return total


def unit(v):
    return v * lax.rsqrt(jnp.sum(v * v, axis=-1, keepdims=True) + 1e-06)


def attach_kernel(x_ref, decay_ref, out_ref, x_scr, decay_scr, sem):
    copies = [
        pltpu.make_async_copy(x_ref, x_scr, sem.at[0]),
        pltpu.make_async_copy(decay_ref, decay_scr, sem.at[1]),
    ]
    for copy in copies:
        copy.start()
    for copy in copies:
        copy.wait()
    columns = x_ref.shape[1] // BLOCK
    for c in range(columns):
        out_ref[c * BLOCK : (c + 1) * BLOCK, :] = x_scr[:, c * BLOCK : (c + 1) * BLOCK]
    rest = decay_scr[...]
    parts = []
    for _ in range(PARTS):
        parts.append(rest.astype(BF16).astype(F32))
        rest = rest - parts[-1]
    parts.append(jnp.zeros((EXTRA - PARTS * rest.shape[0], BLOCK), F32))
    out_ref[columns * BLOCK :, :] = jnp.concatenate(parts, axis=0).astype(BF16)


def attach(x, decay):
    hbm = pl.BlockSpec(memory_space=pltpu.HBM)
    return pl.pallas_call(
        attach_kernel,
        out_shape=jax.ShapeDtypeStruct((x.size // BLOCK + EXTRA, BLOCK), BF16),
        in_specs=[hbm, hbm],
        out_specs=pl.BlockSpec(memory_space=pltpu.VMEM),
        scratch_shapes=[
            pltpu.VMEM(x.shape, BF16),
            pltpu.VMEM(decay.shape, F32),
            pltpu.SemaphoreType.DMA((2,)),
        ],
        compiler_params=pltpu.CompilerParams(vmem_limit_bytes=VMEM_LIMIT),
        name="attach_decay",
    )(x, decay)


def rows_of(ref):
    columns = ref.shape[0] // BLOCK
    return jnp.concatenate([ref[c * BLOCK : (c + 1) * BLOCK, :] for c in range(columns)], axis=1)


def running_decay(parts, head, heads):
    row, col = place_iota()
    upto = jnp.where(row <= col, 1.0, 0.0).astype(BF16)
    line = lax.broadcasted_iota(jnp.int32, parts.shape, 0)
    mine = jnp.where((line % heads == head) & (line < PARTS * heads), parts.astype(F32), 0.0)
    return jnp.sum(mm(mine.astype(BF16), upto), axis=0, keepdims=True)


def block_terms(projs, cums):
    row, col = place_iota()
    hd = BLOCK
    q = [unit(p[:, :hd].astype(BF16).astype(F32)) for p in projs]
    k = [unit(p[:, hd : 2 * hd].astype(BF16).astype(F32)) for p in projs]
    v = [p[:, 2 * hd : 3 * hd].astype(BF16).astype(F32) for p in projs]
    beta = [jax.nn.sigmoid(p[:, 3 * hd :]) for p in projs]
    across = [jnp.broadcast_to(c, (BLOCK, BLOCK)) for c in cums]
    down = [jnp.transpose(a) for a in across]
    kb = [a.astype(BF16) for a in k]
    inner = [
        mm(jnp.concatenate([a.astype(BF16), b], axis=0), b, ((1,), (1,))) for a, b in zip(q, kb)
    ]
    ratio = [
        jnp.where(row >= col, jnp.exp(jnp.where(row >= col, d - a, 0.0)), 0.0)
        for d, a in zip(down, across)
    ]
    negs = [
        jnp.where(row > col, -(b * r * i[BLOCK:]), 0.0) for b, r, i in zip(beta, ratio, inner)
    ]
    growth = [jnp.exp(d) for d in down]
    rhs = [
        jnp.concatenate([b * g * a, b * c], axis=1) for b, g, a, c in zip(beta, growth, k, v)
    ]
    inv = lower_inverse(negs)
    solved = [mm(t.astype(BF16), r.astype(BF16)).astype(BF16) for t, r in zip(inv, rhs)]
    scores = [(i[:BLOCK] * r).astype(BF16) for i, r in zip(inner, ratio)]
    inside = [mm(s, w) for s, w in zip(scores, solved)]
    last = [d[BLOCK - 1 :, :] for d in down]
    tail = [(jnp.exp(e - d) * a).astype(BF16) for e, d, a in zip(last, down, k)]
    step = [mm(w, t, ((0,), (0,))) for w, t in zip(solved, tail)]
    fade = [jnp.exp(e) for e in last]
    reads = [g * a - i[:, :hd] for g, a, i in zip(growth, q, inside)]
    local = [i[:, hd:] for i in inside]
    return reads, local, step, fade


def where_am_i():
    place = lax.axis_index("seq")
    inner = jnp.bitwise_and(place, EXPERTS - 1)
    return place - inner, inner // CORES, jnp.bitwise_and(inner, 1)


def routes(kinds_ref, base):
    kinds = [kinds_ref[base + b] for b in range(EXPERTS)]
    ranks = []
    for b in range(EXPERTS):
        rank = jnp.int32(0)
        for earlier in range(b):
            rank = rank + jnp.where(kinds[earlier] == kinds[b], 1, 0)
        ranks.append(rank)
    return kinds, ranks


def sources(kinds, ranks, kind):
    found = []
    for slot in range(CAP):
        block = jnp.int32(0)
        for b in range(EXPERTS):
            block = block + jnp.where((kinds[b] == kind) & (ranks[b] == slot), b, 0)
        found.append(block)
    return found


def arrivals(chip, core):
    return [
        jnp.bitwise_and(chip + hop, CHIPS - 1) * CORES + (core if side == 0 else 1 - core)
        for hop in HOPS
        for side in (0, 1)
    ]


def normed(x, gain):
    xf = x.astype(F32)
    return (xf * lax.rsqrt(jnp.mean(xf * xf, axis=-1, keepdims=True) + 1e-06) * gain).astype(BF16)


def pair_terms(gain_ref, weight_ref, x_refs, norm_ref, put):
    _, chip, core = where_am_i()
    head = chip * CORES + core
    gain = gain_ref[...]
    columns = x_refs[0].shape[0] // BLOCK
    for j, ref in enumerate(x_refs):
        norm_ref[j * BLOCK : (j + 1) * BLOCK, :] = normed(rows_of(ref), gain)
    both = mm(norm_ref[...], weight_ref[...])
    reads, local, step, fade = block_terms(
        [both[:BLOCK], both[BLOCK:]],
        [running_decay(ref[columns * BLOCK :, :], head, columns) for ref in x_refs],
    )
    for i, spot in ((0, core), (1, 1 - core)):
        put((0, 1), spot, reads[i].astype(BF16), local[i])
    ahead = core == 0
    step = [jnp.where(ahead, step[0], step[1]), jnp.where(ahead, step[1], step[0])]
    fade = [jnp.where(ahead, fade[0], fade[1]), jnp.where(ahead, fade[1], fade[0])]
    first, second = step
    cross = mm3(halves(first), halves(second[:BLOCK]))
    both_move = fade[1] * first[:BLOCK] + fade[0] * second[:BLOCK] - cross[:BLOCK]
    both_add = fade[1] * first[BLOCK:] - cross[BLOCK:] + second[BLOCK:]
    put((2, 3), 0, first, jnp.broadcast_to(fade[0], (8, BLOCK)))
    both_step = jnp.concatenate([both_move, both_add], axis=0)
    put((2, 3), 1, both_step, jnp.broadcast_to(fade[0] * fade[1], (8, BLOCK)))


def term_scratch(count, width):
    return [pltpu.VMEM((count * BLOCK, width), BF16)]


def term_shapes(count):
    return (
        ((count, BLOCK, BLOCK), BF16),
        ((count, BLOCK, BLOCK), F32),
        ((count, 2 * BLOCK, BLOCK), F32),
        ((count, 8, BLOCK), F32),
    )


def terms_kernel(gain_ref, weight_ref, left_ref, right_ref, *refs):
    outs, scratch = refs[:4], refs[4:]

    def put(which, spot, *values):
        for n, value in zip(which, values):
            outs[n][spot] = value

    pair_terms(gain_ref, weight_ref, (left_ref, right_ref), *scratch, put)


def terms(gain, weight, blocks):
    count = len(blocks)
    width = gain.shape[1]
    vmem = pl.BlockSpec(memory_space=pltpu.VMEM)
    return pl.pallas_call(
        terms_kernel,
        out_shape=tuple(jax.ShapeDtypeStruct(*s) for s in term_shapes(count)),
        in_specs=[vmem] * 4,
        out_specs=(vmem,) * 4,
        scratch_shapes=term_scratch(count, width),
        compiler_params=pltpu.CompilerParams(vmem_limit_bytes=VMEM_LIMIT),
        cost_estimate=pl.CostEstimate(
            flops=4 * 10**9, bytes_accessed=3 * 10**6, transcendentals=10**5
        ),
        name="chunk_terms",
    )(gain, weight, *blocks)


def mix_kernel(pairs, late, kinds_ref, out_gain_ref, *refs):
    base, chip, core = where_am_i()
    groups = [refs[4 * g : 4 * g + 4] for g in range(pairs)]
    refs = refs[4 * pairs :]
    if late:
        gain_ref, weight_ref, left_ref, right_ref = refs[:4]
        refs = refs[4:]
    else:
        start_ref, refs = refs[0], refs[1:]
    outs, refs = refs[:CHIPS], refs[CHIPS:]
    scr, on_scr, refs = refs[:4], refs[4], refs[5:]
    for group, hop in zip(groups, HOPS):
        spot = jnp.bitwise_and(chip + hop, CHIPS - 1) * CORES
        for ref, keep in zip(group, scr):
            for i in range(CORES):
                keep[spot + i] = ref[i]
    if late:
        late_spot = jnp.bitwise_and(chip + HOPS[-1], CHIPS - 1) * CORES

        def put(which, spot, *values):
            for n, value in zip(which, values):
                scr[n][late_spot + spot] = value

        pair_terms(gain_ref, weight_ref, (left_ref, right_ref), *refs, put)
    reads_scr, local_scr, step_scr, fade_scr = scr
    state = jnp.zeros((BLOCK, BLOCK), F32) if late else start_ref[...]
    out_gain = out_gain_ref[...]

    def after(split, state, at):
        move = step_scr[at]
        return fade_scr[at][0:1, :] * state - mm3(split, halves(move[:BLOCK])) + move[BLOCK:]

    for c in range(CHIPS):
        at = c * CORES
        split = halves(state)
        between = after(split, state, at)
        if c + 1 < CHIPS:
            state = after(split, state, at + 1)
        for b, before in ((at, split[0]), (at + 1, between.astype(BF16))):
            mixed = mm(reads_scr[b], before, ((1,), (1,))) + local_scr[b]
            on_scr[b] = normed(mixed, out_gain)
    kinds, ranks = routes(kinds_ref, base)
    for k in range(CHIPS):
        there = jnp.bitwise_xor(chip, k)
        for side in range(CORES):
            found = sources(kinds, ranks, there * CORES + side)
            for slot in range(CAP):
                outs[k][side, slot] = on_scr[found[slot]]


def mix(kinds, out_gain, groups, start=None, late=()):
    vmem = pl.BlockSpec(memory_space=pltpu.VMEM)
    extra = list(late) if late else [start]
    operands = [kinds, out_gain] + [a for g in groups for a in g] + extra
    sent = jax.ShapeDtypeStruct((CORES, CAP, BLOCK, BLOCK), BF16)
    return pl.pallas_call(
        partial(mix_kernel, len(groups), bool(late)),
        out_shape=(sent,) * CHIPS,
        in_specs=[pl.BlockSpec(memory_space=pltpu.SMEM)] + [vmem] * (len(operands) - 1),
        out_specs=(vmem,) * CHIPS,
        scratch_shapes=[pltpu.VMEM(*s) for s in term_shapes(EXPERTS)]
        + [pltpu.VMEM((EXPERTS, BLOCK, BLOCK), BF16)]
        + (term_scratch(2, late[0].shape[1]) if late else []),
        compiler_params=pltpu.CompilerParams(vmem_limit_bytes=VMEM_LIMIT),
        cost_estimate=pl.CostEstimate(
            flops=3 * 10**10, bytes_accessed=4 * 10**6, transcendentals=10**5
        ),
        name="state_walk",
    )(*operands)


def home_kernel(kinds_ref, own_ref, other_ref, *outs):
    base, chip, core = where_am_i()
    kinds, ranks = routes(kinds_ref, base)
    for k in range(CHIPS):
        home = jnp.bitwise_and(chip + k, CHIPS - 1) * CORES + core
        kind, rank = jnp.int32(0), jnp.int32(0)
        for b in range(EXPERTS):
            kind = kind + jnp.where(home == b, kinds[b], 0)
            rank = rank + jnp.where(home == b, ranks[b], 0)
        here = kind // CORES == chip
        mine = jnp.bitwise_and(kind, 1) == core
        outs[k][...] = jnp.zeros_like(outs[k])
        for slot in range(CAP):
            rows = slice(slot * BLOCK, (slot + 1) * BLOCK)

            @pl.when(here & mine & (rank == slot))
            def _():
                outs[k][...] = own_ref[rows, :]

            @pl.when(here & jnp.logical_not(mine) & (rank == slot))
            def _():
                outs[k][...] = other_ref[rows, :]


def homeward(kinds, own, other):
    vmem = pl.BlockSpec(memory_space=pltpu.VMEM)
    rows, width = own.shape
    return pl.pallas_call(
        home_kernel,
        out_shape=(jax.ShapeDtypeStruct((rows // CAP, width), BF16),) * CHIPS,
        in_specs=[pl.BlockSpec(memory_space=pltpu.SMEM), vmem, vmem],
        out_specs=(vmem,) * CHIPS,
        compiler_params=pltpu.CompilerParams(vmem_limit_bytes=VMEM_LIMIT),
        name="homeward",
    )(kinds, own, other)


def add_heads(half, out_weight_ref, on_refs, on_scr):
    _, chip, core = where_am_i()
    for k in range(CHIPS // 2):
        there = jnp.bitwise_and(jnp.bitwise_xor(chip, k), 1)
        for side in range(CORES):
            head = there * CORES + (core if side == 0 else 1 - core)
            at = pl.ds(pl.multiple_of(head * BLOCK, BLOCK), BLOCK)
            for slot in range(CAP):
                on_scr[slot * BLOCK : (slot + 1) * BLOCK, at] = on_refs[k * CORES + side][core, slot]
    depth = on_scr.shape[1]
    part = jnp.bitwise_xor(chip // 2, half)
    rows = pl.ds(pl.multiple_of(part * depth, depth), depth)
    return mm(on_scr[...], out_weight_ref[rows, :])


def early_kernel(kinds_ref, out_weight_ref, *refs):
    x_refs, on_refs = refs[:EXPERTS], refs[EXPERTS : EXPERTS + CHIPS]
    out_ref, x_scr, on_scr, sem = refs[EXPERTS + CHIPS :]
    base, chip, core = where_am_i()
    kinds, ranks = routes(kinds_ref, base)
    found = sources(kinds, ranks, chip * CORES + core)
    size = x_scr.shape[1]
    for slot in range(CAP):
        for block, ref in zip(arrivals(chip, core), x_refs):

            @pl.when(block == found[slot])
            def _():
                rows = ref.at[pl.ds(0, size), :]
                pltpu.make_async_copy(rows, x_scr.at[slot], sem.at[slot]).start()

    added = add_heads(0, out_weight_ref, on_refs, on_scr)
    for slot in range(CAP):
        rows = slice(slot * BLOCK, (slot + 1) * BLOCK)
        pltpu.make_async_copy(x_refs[0].at[pl.ds(0, size), :], x_scr.at[slot], sem.at[slot]).wait()
        out_ref[rows, :] = rows_of(x_scr.at[slot]).astype(F32) + added[rows]


def early_project(kinds, out_weight, blocks, ons):
    rows, width = CAP * BLOCK, out_weight.shape[1]
    vmem = pl.BlockSpec(memory_space=pltpu.VMEM)
    return pl.pallas_call(
        early_kernel,
        out_shape=jax.ShapeDtypeStruct((rows, width), F32),
        in_specs=[pl.BlockSpec(memory_space=pltpu.SMEM), vmem]
        + [pl.BlockSpec(memory_space=pl.ANY)] * EXPERTS
        + [vmem] * len(ons),
        out_specs=vmem,
        scratch_shapes=[
            pltpu.VMEM((CAP, width, BLOCK), BF16),
            pltpu.VMEM((rows, width // 2), BF16),
            pltpu.SemaphoreType.DMA((CAP,)),
        ],
        compiler_params=pltpu.CompilerParams(vmem_limit_bytes=VMEM_LIMIT),
        cost_estimate=pl.CostEstimate(flops=0, bytes_accessed=0, transcendentals=0),
        name="early_project",
    )(kinds, out_weight, *blocks, *ons)


def project(gain_ref, out_weight_ref, early_ref, on_refs, on_scr, h_ref, hn_ref):
    hidden = (early_ref[...] + add_heads(1, out_weight_ref, on_refs, on_scr)).astype(BF16)
    h_ref[...] = hidden
    hn_ref[...] = normed(hidden, gain_ref[...])


def project_kernel(gain_ref, out_weight_ref, early_ref, *refs):
    h_ref, hn_ref, on_scr = refs[CHIPS:]
    project(gain_ref, out_weight_ref, early_ref, refs[:CHIPS], on_scr, h_ref, hn_ref)


def expert_kernel(tile, gain_ref, out_weight_ref, early_ref, *refs):
    on_refs = refs[:CHIPS]
    gate_ref, up_ref, down_ref, out_ref = refs[CHIPS : CHIPS + 4]
    on_scr, h_scr, hn_scr, act_scr = refs[CHIPS + 4 :]
    project(gain_ref, out_weight_ref, early_ref, on_refs, on_scr, h_scr, hn_scr)
    rows = hn_scr[...]
    for at in range(0, gate_ref.shape[3], tile):
        part = slice(at, at + tile)
        gate = mm(rows, gate_ref[0, 0, :, part])
        up = mm(rows, up_ref[0, 0, :, part])
        act_scr[:, part] = (gate / (1.0 + jnp.exp(-gate)) * up).astype(BF16)
    width = out_ref.shape[1]
    for at in range(0, width, width // 2):
        part = slice(at, at + width // 2)
        ffn = mm(act_scr[...], down_ref[0, 0, :, part]).astype(BF16).astype(F32)
        out_ref[:, part] = (h_scr[:, part].astype(F32) + ffn).astype(BF16)


def expert(gain, out_weight, early, ons, gate, up, down):
    rows, width = early.shape
    vmem = pl.BlockSpec(memory_space=pltpu.VMEM)
    return pl.pallas_call(
        partial(expert_kernel, min(512, gate.shape[3])),
        out_shape=jax.ShapeDtypeStruct((rows, width), BF16),
        in_specs=[vmem] * (len(ons) + 6),
        out_specs=vmem,
        scratch_shapes=[
            pltpu.VMEM((rows, width // 2), BF16),
            pltpu.VMEM((rows, width), BF16),
            pltpu.VMEM((rows, width), BF16),
            pltpu.VMEM((rows, gate.shape[3]), BF16),
        ],
        compiler_params=pltpu.CompilerParams(vmem_limit_bytes=VMEM_LIMIT),
        name="expert",
    )(gain, out_weight, early, *ons, gate, up, down)


def project_only(gain, out_weight, early, ons):
    rows, width = early.shape
    vmem = pl.BlockSpec(memory_space=pltpu.VMEM)
    return pl.pallas_call(
        project_kernel,
        out_shape=(jax.ShapeDtypeStruct((rows, width), BF16),) * 2,
        in_specs=[vmem] * (len(ons) + 3),
        out_specs=(vmem, vmem),
        scratch_shapes=[pltpu.VMEM((rows, width // 2), BF16)],
        compiler_params=pltpu.CompilerParams(vmem_limit_bytes=VMEM_LIMIT),
        name="project",
    )(gain, out_weight, early, *ons)


def group_start(place, count, groups_of_terms):
    groups = count // EXPERTS
    ein = partial(jnp.einsum, precision=lax.Precision.HIGHEST)
    eye = jnp.eye(BLOCK, dtype=F32)
    step = jnp.stack([g[2][1] for g in groups_of_terms], axis=0)
    fade = jnp.stack([g[3][1] for g in groups_of_terms], axis=0)
    chip = place % EXPERTS // CORES
    order = jnp.argsort((chip + jnp.array(HOPS)) % CHIPS)
    step, fade = jnp.take(step, order, axis=0), jnp.take(fade, order, axis=0)
    moves = fade[:, 0, :][:, None, :] * eye - step[:, :BLOCK]
    adds = step[:, BLOCK:]
    total, added = moves[0], adds[0]
    for b in range(1, CHIPS):
        total, added = ein("ij,jk->ik", total, moves[b]), ein("vk,kj->vj", added, moves[b]) + adds[b]
    peers = [[g * EXPERTS + e for g in range(groups)] for e in range(EXPERTS)]
    gather = partial(lax.all_gather, axis_name="seq", axis_index_groups=peers)
    totals, addeds = gather(total), gather(added)

    def one(hop, state):
        return ein(
            "vk,kj->vj", state, lax.dynamic_index_in_dim(totals, hop, 0, False)
        ) + lax.dynamic_index_in_dim(addeds, hop, 0, False)

    return lax.fori_loop(0, place // EXPERTS, one, jnp.zeros((BLOCK, BLOCK), F32))


def per_device(
    held,
    log_decay,
    route_ids,
    norm_gain,
    qkv_weight,
    beta_weight,
    out_gain,
    out_weight,
    ffn_gain,
    gate_weight,
    up_weight,
    down_weight,
):
    count = lax.axis_size("seq")
    sections = lax.axis_size("segment")
    groups = count // EXPERTS
    place = lax.axis_index("seq")
    inner = place % EXPERTS
    width = held.shape[2]
    pair = partial(lax.ppermute, axis_name="seq", perm=pair_route(count))
    kinds = route_ids.reshape(-1)

    def hop(block, by):
        return lax.ppermute(block, "seq", lane_route(count, by))

    own = attach(held[0], log_decay[0].T)
    left = hop(own, 1)
    right = hop(own, -1)
    own_other = pair(own)

    def head_columns(at):
        return lax.dynamic_slice_in_dim(qkv_weight[0], at * width + inner * BLOCK, BLOCK, 1)

    beta_column = lax.dynamic_slice_in_dim(beta_weight[0], inner, 1, 1)
    weight = jnp.concatenate(
        [head_columns(0), head_columns(1), head_columns(2)]
        + [jnp.broadcast_to(beta_column, (width, BLOCK))],
        axis=1,
    )

    known = [terms(norm_gain, weight, (own, own_other))]
    right, _ = lax.optimization_barrier((right, known[0][0]))
    far = hop(right, -1)
    left, _ = lax.optimization_barrier((left, right))
    near = [(own, own_other), (left, pair(left))]
    known.append(terms(norm_gain, weight, near[1]))
    near.append((right, pair(right)))
    known.append(terms(norm_gain, weight, near[2]))
    far, *_ = lax.optimization_barrier((far, known[1][0], known[2][0]))
    last = (far, pair(far))
    if groups > 1:
        known.append(terms(norm_gain, weight, last))
        sends = mix(kinds, out_gain, known, start=group_start(place, count, known))
    else:
        sends = mix(kinds, out_gain, known, late=(norm_gain, weight, *last))

    got = [sends[0], None, None, None]
    for k in (3, 2, 1):
        got[k] = lax.ppermute(sends[k], "seq", chip_route(count, k))
    blocks = [block for two in near + [last] for block in two]
    near_heads = [got[0], pair(got[0]), got[1], pair(got[1])]
    early = early_project(kinds, out_weight[0], blocks, near_heads)
    far_heads = [got[2], pair(got[2]), got[3], pair(got[3])]

    if groups == 1:
        finished = expert(
            ffn_gain, out_weight[0], early, far_heads, gate_weight, up_weight, down_weight
        )
    else:
        hidden, hn = project_only(ffn_gain, out_weight[0], early, far_heads)
        peers = [[g * EXPERTS + e for g in range(groups)] for e in range(EXPERTS)]
        rows = lax.all_gather(hn, "seq", axis_index_groups=peers, tiled=True)
        gate = jnp.dot(rows, gate_weight[0, 0], preferred_element_type=F32)
        up = jnp.dot(rows, up_weight[0, 0], preferred_element_type=F32)
        act = (jax.nn.silu(gate) * up).astype(BF16)
        part = jnp.dot(act, down_weight[0, 0], preferred_element_type=F32)
        ffn = lax.psum_scatter(
            part, "seq", scatter_dimension=0, axis_index_groups=peers, tiled=True
        ).astype(BF16)
        finished = (hidden.astype(F32) + ffn.astype(F32)).astype(BF16)

    def send_home(block, by):
        return lax.ppermute(block, ("segment", "seq"), home_route(sections, count, by))

    here, right_home, far_home, left_home = homeward(kinds, finished, pair(finished))
    passed = hop(far_home, -1)
    from_right = send_home(right_home, 1)
    from_here = send_home(here, 0)
    from_left = send_home(passed + left_home, -1)
    return (from_left + from_right + from_here)[None]


def solution(mesh):
    placed = (
        P("segment", "seq", None),
        P("segment", "seq", None),
        P("segment", None, None),
        P("segment", None),
        P("segment", None, None),
        P("segment", None, None),
        P("segment", None),
        P("segment", None, None),
        P("segment", None),
        P("segment", "seq", None, None),
        P("segment", "seq", None, None),
        P("segment", "seq", None, None),
    )
    return jax.shard_map(
        per_device, mesh=mesh, in_specs=placed, out_specs=P("segment", "seq", None), check_vma=False
    )
```
